256 devices in a mesh: lat: 32 (over y, x, core), lev: 8 (over z).
Axes of the slice: x: 4, y: 4, z: 8, core: 2. Of those that a mesh axis runs over, the one named last changes fastest.
Arguments:
- innovation: float32 [8, 1280, 2560], P('lev', 'lat'), may hold values from -6 to 6
- obs_mask: int32 [8, 1280, 2560], P('lev', 'lat'), may hold values 0 or 1
- obs_weight: float32 [8, 1280, 2560], P('lev', 'lat'), may hold values from 0.25 to 4
- order: int32 [1280], replicated, may hold values from 0 to 1279, each once
- basis: bfloat16 [1280, 640, 1280], P(('lat', 'lev')), may hold values from -0.15625 to 0.15625
- spread: float32 [8, 1280], replicated, may hold values from 0.25 to 2.5
Outputs:
- control: float32 [1280, 16, 1280], P(('lat', 'lev'))
- increment: float32 [8, 1280, 2560], P('lev', 'lat')
The draws below stay inside these ranges and needn't reach their ends.
Inputs may be any that keep to these rules, and one draw needn't show every extreme that they name: order holds every wavenumber once.
All inputs are finite; a program needn't handle non-finite values. No bound on the sum of `obs_mask` on one device may be relied on, other than what follows from the above.
Results may differ from the reference program's by a relative error of at most 0.02.
Values may be sent and summed in bfloat16 or wider, within the bound.
No kernel may reach another device: no remote copies, remote signals or barrier semaphores. Data moves between devices by JAX's collectives and lax.ppermute only.
A program may use at most 128 MiB of HBM per device.

```python
import math
import jax
import jax.numpy as jnp
from jax import lax

NLON = 2560
NLAT = 1280
ITERS = 2
M = 1280
NDEG = 1280
NH = 640
L = 8


def touch_ends(array, stream_key, low, high):
    index_at = [jax.random.randint(jax.random.fold_in(stream_key, axis), (), 0, length) for axis, length in enumerate(array.shape)]
    widest = array.shape.index(max(array.shape))
    next_to = index_at[:widest] + [(index_at[widest] + 1) % array.shape[widest]] + index_at[widest + 1:]
    return array.at[tuple(index_at)].set(low).at[tuple(next_to)].set(high)


def shard_levels(own_key, extent, shards, least, largest):
    def one(dim, parts):
        steps = jax.random.uniform(jax.random.fold_in(jax.random.fold_in(own_key, 6), dim), (parts,), jnp.float32, least / len(shards), largest / len(shards))
        return jnp.repeat(jnp.exp(steps), extent[dim] // parts).reshape((-1,) + (1,) * (len(extent) - dim - 1))

    gain = one(*shards[0])
    for cut in shards[1:]:
        gain = gain * one(*cut)
    return gain


def noise(own_key, extent, width, most, cuts=(), held_as=jnp.bfloat16):
    values = jax.random.normal(own_key, extent, jnp.float32) * width
    if len(cuts) > 0:
        values = shard_levels(own_key, extent, cuts, -0.22, 0.18) * values
    return jnp.clip(values, min=-most, max=most).astype(held_as)


def setup_inputs(seed: int = 0) -> dict:
    keys = jax.random.split(jax.random.key(seed), 7)
    return {
        "innovation": noise(keys[0], (L, NLAT, NLON), 1.0, 6.0, ((0, 8), (1, 32)), jnp.float32),
        "obs_mask": touch_ends((jax.random.randint(keys[1], (L, NLAT, NLON), 0, 2) < 1).astype(jnp.int32), jax.random.fold_in(keys[1], 1), 0, 1),
        "obs_weight": jnp.clip(jnp.exp(math.log(4.0) - 2.7725887 * jax.random.uniform(keys[2], (L, NLAT, NLON), jnp.float32) ** shard_levels(keys[2], (L, NLAT, NLON), ((0, 8), (1, 32)), -0.2, 0.2)), 0.25, 4.0),
        "order": jax.random.permutation(keys[3], M).astype(jnp.int32),
        "basis": noise(keys[4], (M, NH, NDEG), NLAT ** -0.5, 0.15625, ((0, 256),)),
        "spread": jnp.clip(jnp.exp(jax.random.uniform(keys[5], (L, NDEG), jnp.float32, math.log(0.25), math.log(2.5))), 0.25, 2.5),
    }


def wave_table(order):
    longitude = jnp.arange(NLON, dtype=jnp.int32)
    phase = longitude[:, None] * order.astype(jnp.int32)[None, :] % NLON
    angle = phase.astype(jnp.float32) * jnp.float32(2.0 * math.pi / NLON)
    factor = jnp.float32(math.sqrt(2.0 / NLON))
    return (jnp.stack([jnp.cos(angle), jnp.sin(angle)], axis=2) * factor).reshape(NLON, 2 * M).astype(jnp.bfloat16)

def split_parts(values):
    high_part = values.astype(jnp.bfloat16)
    low_part = (values - high_part.astype(jnp.float32)).astype(jnp.bfloat16)
    return (high_part, low_part)

def parity(order):
    degree = jnp.arange(NDEG, dtype=jnp.int32)
    offset = degree[None, :] - order.astype(jnp.int32)[:, None]
    return jnp.where(offset >= 0, jnp.where(offset % 2 == 0, 1.0, -1.0), 0.0).astype(jnp.float32)

def synthesis(control, basis, parity_sign, spread_rows, wave):
    live_mask = jnp.abs(parity_sign)
    scaled = (control * spread_rows[None] * live_mask[:, None, :]).astype(jnp.bfloat16)
    zero_value = jnp.zeros((), jnp.bfloat16)

    def one_slot(item):
        basis_rows, slot_part, slot_sign = item
        even_part = jnp.where(slot_sign[None, :] > 0, slot_part, zero_value)
        odd_part = jnp.where(slot_sign[None, :] < 0, slot_part, zero_value)
        even_sum = jnp.dot(basis_rows, even_part.T, preferred_element_type=jnp.float32)
        odd_sum = jnp.dot(basis_rows, odd_part.T, preferred_element_type=jnp.float32)
        return jnp.concatenate([even_sum + odd_sum, (even_sum - odd_sum)[::-1]], axis=0)
    fourier = lax.map(one_slot, (basis, scaled, parity_sign)).astype(jnp.bfloat16)
    flat_rows = fourier.reshape(M, NLAT, 2, L).transpose(3, 1, 0, 2).reshape(L * NLAT, 2 * M)
    grid_field = jnp.dot(flat_rows, wave.T, preferred_element_type=jnp.float32)
    return grid_field.reshape(L, NLAT, NLON)

def analysis(grid_field, basis, parity_sign, spread_rows, wave):
    grid_hi, grid_lo = split_parts(grid_field.reshape(L * NLAT, NLON))
    spectral_in = jnp.dot(grid_hi, wave, preferred_element_type=jnp.float32) + jnp.dot(grid_lo, wave, preferred_element_type=jnp.float32)
    spectral_in = spectral_in.astype(jnp.bfloat16)
    spectral_in = spectral_in.reshape(L, NLAT, M, 2).transpose(2, 1, 3, 0).reshape(M, NLAT, 2 * L)

    def one_slot(item):
        basis_rows, slot_part, slot_sign = item
        north_part = slot_part[:NH]
        south_part = slot_part[NH:][::-1]
        north_sum = jnp.dot(basis_rows.T, north_part, preferred_element_type=jnp.float32).T
        south_sum = jnp.dot(basis_rows.T, south_part, preferred_element_type=jnp.float32).T
        return north_sum * jnp.abs(slot_sign)[None, :] + slot_sign[None, :] * south_sum
    return lax.map(one_slot, (basis, spectral_in, parity_sign)) * spread_rows[None]

def reference(innovation, obs_mask, obs_weight, order, basis, spread):
    wave = wave_table(order)
    parity_sign = parity(order)
    spread_rows = jnp.tile(spread, (2, 1))
    obs_scale = obs_mask.astype(jnp.float32) * obs_weight

    def hessian(vector):
        return vector + analysis(obs_scale * synthesis(vector, basis, parity_sign, spread_rows, wave), basis, parity_sign, spread_rows, wave)
    rhs = analysis(obs_scale * innovation, basis, parity_sign, spread_rows, wave)
    control = jnp.zeros_like(rhs)
    residual = rhs
    direction = rhs
    norm_now = jnp.sum(residual * residual)
    for turn in range(ITERS):
        hessian_out = hessian(direction)
        step_size = norm_now / jnp.sum(direction * hessian_out)
        control = control + step_size * direction
        residual = residual - step_size * hessian_out
        norm_next = jnp.sum(residual * residual)
        direction = residual + norm_next / norm_now * direction
        norm_now = norm_next
    increment = synthesis(control, basis, parity_sign, spread_rows, wave)
    return (control, increment)
```

```python
import functools
import math

import jax
import jax.numpy as jnp
from jax import lax
from jax.experimental import pallas as pl
from jax.experimental.pallas import tpu as pltpu
from jax.sharding import PartitionSpec as P

BF = jnp.bfloat16
F32 = jnp.float32
GROUPS = 3
SUB = 4
SPARE = 120
VMEM_LIMIT = 40 * 1024 * 1024


def iota(shape, axis):
    return lax.broadcasted_iota(jnp.int32, shape, axis)


def params():
    return pltpu.CompilerParams(vmem_limit_bytes=VMEM_LIMIT)


def mm(a, b):
    return jnp.dot(a, b, preferred_element_type=F32)


def mm_nt(a, b):
    return lax.dot_general(a, b, (((1,), (1,)), ((), ())), preferred_element_type=F32)


def pack_scalars(values):
    lane = iota((1, 128), 1)
    out = jnp.zeros((1, 128), F32)
    for index, value in enumerate(values):
        rest = jnp.zeros((1, 128), F32) + value
        for piece in range(3):
            part = rest.astype(BF).astype(F32)
            rest = rest - part
            out = jnp.where(lane == SPARE + 3 * index + piece, part, out)
    return out


def unpack_scalars(received, count):
    total = jnp.sum(received, axis=0, keepdims=True) * (1.0 / SUB)
    lane = iota((1, 128), 1)
    sums = []
    for index in range(count):
        first = SPARE + 3 * index
        sums.append(jnp.sum(jnp.where((lane >= first) & (lane < first + 3), total, 0.0)))
    return sums


def make_rhs(field, south, rows, half):
    high = field.astype(BF).astype(F32)
    low = field - high
    gap = jnp.zeros((64 - rows, half), F32)
    stacked = jnp.concatenate(
        [high[:, :half], gap, low[:, :half], gap, high[:, half:], gap, low[:, half:], gap], axis=0
    ).astype(BF)
    to = iota((256, 256), 0)
    source = iota((256, 256), 1)
    inner = to & 63
    flipped = jnp.where((south > 0) & (inner < rows), to - inner + (rows - 1) - inner, to)
    chooser = jnp.where(source == flipped, 1.0, 0.0).astype(BF)
    return mm(chooser, stacked).astype(BF)


def project(table, rhs, sign):
    product = mm_nt(table, rhs)
    both = product[:, :128] + sign * product[:, 128:]
    return both + pltpu.roll(both, 64, 1)


def column(cols, group):
    picked = cols[:, 0:1]
    for index in range(1, GROUPS):
        picked = jnp.where(group == index, cols[:, index : index + 1], picked)
    return picked


def first_kernel(rows, points, south_ref, cols_ref, inn_ref, mask_ref, weight_ref, table_ref, send_ref, rhs_ref, acc_ref):
    half = points // 2
    block = pl.program_id(0)
    group = pl.program_id(1)

    @pl.when((block == 0) & (group == 0))
    def _():
        scale = mask_ref[...].astype(F32) * weight_ref[...]
        rhs_ref[...] = make_rhs(scale * inn_ref[...], south_ref[0], rows, half)

    waves = column(cols_ref[...], group)
    count = waves.shape[0]
    place = iota((count, 1), 0) & (SUB - 1)
    valid = (group < GROUPS - 1) | (place < 2)
    factor = jnp.where(valid, math.sqrt(2.0 / points), 0.0)
    turn = (place & 1).astype(F32) * (points // 4)
    wave_f = waves.astype(F32)
    lane = iota((1, 128), 1).astype(F32)

    def cosine(raw):
        inside = raw - jnp.floor((raw + 0.5) * (1.0 / points)) * points
        angle = (jnp.abs(inside - points // 2) - points // 4) * (2.0 * math.pi / points)
        square = angle * angle
        poly = jnp.full_like(square, -1.0 / 39916800.0)
        for coefficient in (1.0 / 362880.0, -1.0 / 5040.0, 1.0 / 120.0, -1.0 / 6.0, 1.0):
            poly = poly * square + coefficient
        return poly * angle

    before = cosine(wave_f * lane - turn) * factor
    now = cosine(wave_f * (lane + 128.0) - turn) * factor
    twice = 2.0 * cosine(wave_f * 128.0)
    pieces = [before.astype(BF), now.astype(BF)]
    for _ in range(2, half // 128):
        before, now = now, twice * now - before
        pieces.append(now.astype(BF))
    for index, piece in enumerate(pieces):
        table_ref[:, 128 * index : 128 * (index + 1)] = piece
    sign = 1.0 - 2.0 * (waves & 1).astype(F32)
    placed = pltpu.roll(project(table_ref[...], rhs_ref[...], sign), group * rows, 1)
    lanes = iota((1, 128), 1)
    mine = (lanes >= group * rows) & (lanes < (group + 1) * rows)
    acc = jnp.where(mine, placed, jnp.where(group == 0, 0.0, acc_ref[...]))
    acc_ref[...] = acc

    @pl.when(group == GROUPS - 1)
    def _():
        send_ref[...] = acc.astype(BF)


def grid_synthesis(south, received, table_ref, copies, mrows, rows, points):
    half = points // 2
    source = iota((128, 128), 0)
    to = iota((128, 128), 1)
    base = jnp.where(to >= 2 * rows, 2 * rows, jnp.where(to >= rows, rows, 0))
    flipped = jnp.where((south > 0) & (to < SPARE), 2 * base + (rows - 1) - to, to)
    chooser = jnp.where((source == flipped) & (to < SPARE), 1.0, 0.0).astype(BF)
    across = mm(received, chooser).T
    signs = 1.0 - 2.0 * (mrows & 1).astype(F32)
    total = jnp.zeros((2 * rows, half), F32)
    per_group = received.shape[0]
    step = per_group * GROUPS // len(copies)
    for group in range(GROUPS):
        lines = across[rows * group : rows * (group + 1)]
        lhs = jnp.concatenate([lines, lines * signs[group : group + 1]], axis=0).astype(BF)
        for part in range(per_group // step):
            index = group * (per_group // step) + part
            copies[index].wait()
            total = total + mm(lhs[:, part * step : (part + 1) * step], table_ref[index * step : (index + 1) * step, :])
    return jnp.concatenate([total[:rows], total[rows:]], axis=1)


def start_copies(hbm_ref, vmem_ref, sems, count):
    step = hbm_ref.shape[0] // count
    copies = []
    for index in range(count):
        window = pl.ds(index * step, step)
        copies.append(pltpu.make_async_copy(hbm_ref.at[window], vmem_ref.at[window], sems.at[index]))
        copies[-1].start()
    return copies


def middle_kernel(rows, points, south_ref, x_ref, table_hbm, cols_ref, mrows_ref, mask_ref, weight_ref,
                  field_ref, send_ref, scalar_ref, table_ref, rhs_ref, sems):
    half = points // 2
    copies = start_copies(table_hbm, table_ref, sems, 6)
    received = x_ref[...]
    (norm0,) = unpack_scalars(received.astype(F32), 1)
    field = grid_synthesis(south_ref[0], received, table_ref, copies, mrows_ref[...], rows, points)
    field_ref[...] = field
    scaled = mask_ref[...].astype(F32) * weight_ref[...] * field
    energy = jnp.sum(scaled * field)
    rhs_ref[...] = make_rhs(scaled, south_ref[0], rows, half)
    scalar_ref[...] = jnp.zeros((8, 128), F32) + norm0
    extra = pack_scalars([norm0, energy])
    lanes = iota((1, 128), 1)
    per_group = x_ref.shape[0]
    step = 256

    def body(block, carry):
        start = pl.multiple_of(block * step, step)
        cols = cols_ref[pl.ds(start, step), :]
        acc = jnp.zeros((step, 128), F32) + extra
        for group in range(GROUPS):
            sign = 1.0 - 2.0 * (cols[:, group : group + 1] & 1).astype(F32)
            lines = table_ref[pl.ds(pl.multiple_of(group * per_group + block * step, step), step), :]
            placed = project(lines, rhs_ref[...], sign)
            if group > 0:
                placed = pltpu.roll(placed, group * rows, 1)
            acc = jnp.where((lanes >= group * rows) & (lanes < (group + 1) * rows), placed, acc)
        send_ref[pl.ds(start, step), :] = acc.astype(BF)
        return carry

    lax.fori_loop(0, per_group // step, body, 0)


def last_kernel(rows, points, south_ref, x_ref, table_hbm, mrows_ref, mask_ref, weight_ref, first_ref, scalar_in,
                field_ref, energy_ref, scalar_ref, table_ref, sems):
    copies = start_copies(table_hbm, table_ref, sems, 6)
    received = x_ref[...]
    norm1, cross = unpack_scalars(received.astype(F32), 2)
    norm0 = scalar_in[0:1, 0:1]
    beta = (jnp.zeros((1, 1), F32) + norm1) / norm0
    field = grid_synthesis(south_ref[0], received, table_ref, copies, mrows_ref[...], rows, points)
    field = field + beta * first_ref[...]
    field_ref[...] = field
    scaled = mask_ref[...].astype(F32) * weight_ref[...] * field
    energy_ref[...] = jnp.zeros(energy_ref.shape, F32) + jnp.sum(scaled * field)
    line = iota((8, 128), 0)
    scalar_ref[...] = jnp.where(line == 0, norm1, cross)


def lane_windows(band, rows):
    start = band * rows
    block, offset = start // 128, start % 128
    if offset + rows <= 128:
        return [(block, offset, offset + rows)]
    return [(block, offset, 128), (block + 1, 0, offset + rows - 128)]


def chooser(part, transposed):
    shape = (64, 32) if transposed else (32, 64)
    fine = iota(shape, 1 if transposed else 0)
    wide = iota(shape, 0 if transposed else 1)
    where = (fine >> 4) * 32 + (fine & 7) * SUB + 2 * part + ((fine >> 3) & 1)
    return jnp.where(wide == where, 1.0, 0.0).astype(BF)


def parity_row(wave, degrees):
    offset = iota((1, degrees), 1) - wave
    return jnp.where(offset >= 0, 1.0 - 2.0 * (offset & 1).astype(F32), 0.0)


def spectral_kernel(rows, with_base, waves_ref, x_ref, basis_hbm, spread_ref, *refs):
    if with_base:
        base_ref, out_ref, send_ref, scalar_ref, basis_ref, sems = refs
    else:
        out_ref, send_ref, scalar_ref, basis_ref, sems = refs
    owned, half_rows, degrees = basis_hbm.shape
    bands = half_rows // rows
    copies = start_copies(basis_hbm, basis_ref, sems, owned)
    received = x_ref[...].astype(F32)
    lane = iota((1, 128), 1)
    if with_base:
        norm0, energy = unpack_scalars(received, 2)
        norm0 = (jnp.zeros((1, 1), F32) + norm0) * (1.0 / (2 * bands * 8))
        step_size = norm0 / (norm0 + energy)
        scalar_ref[...] = jnp.zeros((8, 128), F32) + step_size
    spread_rows = jnp.concatenate([spread_ref[...], spread_ref[...]], axis=0)
    blocks = half_rows // 128
    lines = []
    for group in range(GROUPS):
        parts = []
        for side in range(2):
            columns = [jnp.zeros((32, 128), F32)] * blocks
            for band in range(bands):
                row = band if side == 0 else 2 * bands - 1 - band
                block = received[32 * row : 32 * row + 32]
                shift = (rows * band - rows * group) % 128
                if shift:
                    block = pltpu.roll(block, shift, 1)
                for index, low, high in lane_windows(band, rows):
                    columns[index] = jnp.where((lane >= low) & (lane < high), block, columns[index])
            parts.append(jnp.concatenate(columns, axis=1))
        lines.append(jnp.concatenate(parts, axis=0).astype(BF))
    norm = jnp.zeros((1, 1), F32)
    cross = jnp.zeros((1, 1), F32)
    parities = []
    for slot in range(owned):
        parity = parity_row(waves_ref[slot], degrees)
        parities.append(parity)
        lhs = mm(chooser(slot % 2, False), lines[slot // 2]).astype(BF)
        copies[slot].wait()
        sums = mm(lhs, basis_ref[slot])
        value = (sums[:16] * jnp.abs(parity) + parity * sums[16:]) * spread_rows
        if with_base:
            base = base_ref[slot]
            value = base - step_size * (base + value)
            cross = cross + jnp.sum(value * base)
        out_ref[slot] = value
        norm = norm + jnp.sum(value * value)
    if with_base:
        extra = pack_scalars([norm, cross])
    else:
        extra = pack_scalars([norm])
        scalar_ref[...] = jnp.zeros((8, 128), F32)
    wide = [None] * GROUPS
    for slot in range(owned):
        parity = parities[slot]
        coeff = (out_ref[slot] * spread_rows * jnp.abs(parity)).astype(BF).astype(F32)
        even = jnp.where(parity > 0, coeff, 0.0)
        odd = jnp.where(parity < 0, coeff, 0.0)
        sums = mm_nt(jnp.concatenate([even, odd], axis=0).astype(BF), basis_ref[slot])
        sides = jnp.concatenate([sums[:16] + sums[16:], sums[:16] - sums[16:]], axis=0).astype(BF)
        spreaded = mm(chooser(slot % 2, True), sides)
        group = slot // 2
        wide[group] = spreaded if wide[group] is None else wide[group] + spreaded
    for side in range(2):
        for band in range(bands):
            block = jnp.zeros((32, 128), F32) + extra
            for group in range(GROUPS):
                shift = (rows * group - rows * band) % 128
                place = rows * group
                for index, low, high in lane_windows(band, rows):
                    source = wide[group][32 * side : 32 * side + 32, 128 * index : 128 * index + 128]
                    if shift:
                        source = pltpu.roll(source, shift, 1)
                    block = jnp.where((lane >= place) & (lane < place + high - low), source, block)
                    place += high - low
            row = band if side == 0 else 2 * bands - 1 - band
            send_ref[32 * row : 32 * row + 32, :] = block.astype(BF)


SMEM = pl.BlockSpec(memory_space=pltpu.SMEM)
VMEM = pl.BlockSpec(memory_space=pltpu.VMEM)
ANY = pl.BlockSpec(memory_space=pl.ANY)


def shape(dims, dtype):
    return jax.ShapeDtypeStruct(dims, dtype)


def exchange(buffer):
    return lax.all_to_all(buffer, ("lat", "lev"), split_axis=0, concat_axis=0, tiled=True)


def local(innovation, obs_mask, obs_weight, order, basis, spread):
    lat = lax.axis_index("lat")
    lev = lax.axis_index("lev")
    devices = lax.axis_size("lat") * lax.axis_size("lev")
    owned, half_rows, degrees = basis.shape
    rows, points = innovation.shape[1:]
    half = points // 2
    chunk_rows = devices * SUB
    table_rows = GROUPS * chunk_rows
    mask = obs_mask.reshape(rows, points)
    weight = obs_weight.reshape(rows, points)
    south = (lat >= lax.axis_size("lat") // 2).astype(jnp.int32).reshape(1)
    my_waves = lax.dynamic_slice_in_dim(order, (lat * lax.axis_size("lev") + lev) * owned, owned)
    slots = jnp.pad(order.reshape(devices, owned), ((0, 0), (0, 2 * GROUPS - owned))).reshape(devices, GROUPS, 2)
    cols = jnp.repeat(slots.transpose(0, 2, 1), 2, axis=1).reshape(chunk_rows, GROUPS)
    mrows = jnp.pad(cols.T, ((0, 8 - GROUPS), (0, 0)))

    blocks = chunk_rows // 256
    table, send = pl.pallas_call(
        functools.partial(first_kernel, rows, points),
        grid=(blocks, GROUPS),
        in_specs=[
            SMEM,
            pl.BlockSpec((256, GROUPS), lambda b, g: (b, 0)),
            pl.BlockSpec((rows, points), lambda b, g: (0, 0)),
            pl.BlockSpec((rows, points), lambda b, g: (0, 0)),
            pl.BlockSpec((rows, points), lambda b, g: (0, 0)),
        ],
        out_specs=[
            pl.BlockSpec((256, half), lambda b, g: (g * blocks + b, 0)),
            pl.BlockSpec((256, 128), lambda b, g: (b, 0)),
        ],
        out_shape=[shape((table_rows, half), BF), shape((chunk_rows, 128), BF)],
        scratch_shapes=[pltpu.VMEM((256, half), BF), pltpu.VMEM((256, 128), F32)],
        compiler_params=params(),
        name="first",
    )(south, cols, innovation.reshape(rows, points), mask, weight)

    def spectral(received, base):
        with_base = base is not None
        return pl.pallas_call(
            functools.partial(spectral_kernel, rows, with_base),
            in_specs=[SMEM, VMEM, ANY, VMEM] + [VMEM] * with_base,
            out_specs=[VMEM] * 3,
            out_shape=[shape((owned, 16, degrees), F32), shape((chunk_rows, 128), BF), shape((8, 128), F32)],
            scratch_shapes=[pltpu.VMEM(basis.shape, BF), pltpu.SemaphoreType.DMA((owned,))],
            compiler_params=params(),
            name="spectral",
        )(my_waves, received, basis, spread, *([base] * with_base))

    rhs, send, _ = spectral(exchange(send), None)
    field1, send, norm0 = pl.pallas_call(
        functools.partial(middle_kernel, rows, points),
        in_specs=[SMEM, VMEM, ANY, VMEM, VMEM, VMEM, VMEM],
        out_specs=[VMEM] * 3,
        out_shape=[shape((rows, points), F32), shape((chunk_rows, 128), BF), shape((8, 128), F32)],
        scratch_shapes=[
            pltpu.VMEM((table_rows, half), BF),
            pltpu.VMEM((256, half), BF),
            pltpu.SemaphoreType.DMA((6,)),
        ],
        compiler_params=params(),
        name="middle",
    )(south, exchange(send), table, cols, mrows, mask, weight)
    residual, send, step1 = spectral(exchange(send), rhs)
    field2, energy, norms = pl.pallas_call(
        functools.partial(last_kernel, rows, points),
        in_specs=[SMEM, VMEM, ANY, VMEM, VMEM, VMEM, VMEM, VMEM],
        out_specs=[VMEM] * 3,
        out_shape=[shape((rows, points), F32), shape((devices, 128), F32), shape((8, 128), F32)],
        scratch_shapes=[pltpu.VMEM((table_rows, half), BF), pltpu.SemaphoreType.DMA((6,))],
        compiler_params=params(),
        name="last",
    )(south, exchange(send), table, mrows, mask, weight, field1, norm0)
    total = jnp.sum(exchange(energy)[:, 0])
    first = norm0[0, 0]
    norm1 = norms[0, 0]
    cross = norms[1, 0]
    beta = norm1 / first
    alpha1 = step1[0, 0]
    alpha2 = norm1 / (norm1 + 2.0 * beta * cross + beta * beta * first + total)
    control = alpha1 * rhs + alpha2 * (residual + beta * rhs)
    increment = alpha1 * field1 + alpha2 * field2
    return (control, increment.reshape(innovation.shape))


def solution(mesh):
    in_specs = (
        P("lev", "lat", None),
        P("lev", "lat", None),
        P("lev", "lat", None),
        P(),
        P(("lat", "lev"), None, None),
        P(),
    )
    out_specs = (P(("lat", "lev"), None, None), P("lev", "lat", None))
    return jax.shard_map(local, mesh=mesh, in_specs=in_specs, out_specs=out_specs, check_vma=False)
```

```python
import functools
import math

import jax
import jax.numpy as jnp
from jax import lax
from jax.experimental import pallas as pl
from jax.experimental.pallas import tpu as pltpu
from jax.sharding import PartitionSpec as P

BF = jnp.bfloat16
F32 = jnp.float32
GROUPS = 3
SUB = 4
SPARE = 120
VMEM_LIMIT = 20 * 1024 * 1024


def iota(shape, axis):
    return lax.broadcasted_iota(jnp.int32, shape, axis)


def params():
    return pltpu.CompilerParams(vmem_limit_bytes=VMEM_LIMIT)


def mm(a, b):
    return jnp.dot(a, b, preferred_element_type=F32)


def mm_nt(a, b):
    return lax.dot_general(a, b, (((1,), (1,)), ((), ())), preferred_element_type=F32)


def pack_scalars(values):
    lane = iota((1, 128), 1)
    out = jnp.zeros((1, 128), F32)
    for index, value in enumerate(values):
        rest = jnp.zeros((1, 128), F32) + value
        for piece in range(3):
            part = rest.astype(BF).astype(F32)
            rest = rest - part
            out = jnp.where(lane == SPARE + 3 * index + piece, part, out)
    return out


def unpack_scalars(received, count):
    total = jnp.sum(received, axis=0, keepdims=True) * (1.0 / SUB)
    lane = iota((1, 128), 1)
    sums = []
    for index in range(count):
        first = SPARE + 3 * index
        sums.append(jnp.sum(jnp.where((lane >= first) & (lane < first + 3), total, 0.0)))
    return sums


def make_rhs(field, south, rows, half):
    high = field.astype(BF).astype(F32)
    low = field - high
    gap = jnp.zeros((64 - rows, half), F32)
    stacked = jnp.concatenate(
        [high[:, :half], gap, low[:, :half], gap, high[:, half:], gap, low[:, half:], gap], axis=0
    ).astype(BF)
    to = iota((256, 256), 0)
    source = iota((256, 256), 1)
    inner = to & 63
    flipped = jnp.where((south > 0) & (inner < rows), to - inner + (rows - 1) - inner, to)
    chooser = jnp.where(source == flipped, 1.0, 0.0).astype(BF)
    return mm(chooser, stacked).astype(BF)


def project(table, rhs, sign):
    product = mm_nt(table, rhs)
    both = product[:, :128] + sign * product[:, 128:]
    return both + pltpu.roll(both, 64, 1)


def circle(steps, points):
    quarter = points // 4
    turns = jnp.floor(steps * (1.0 / quarter) + 0.5)
    angle = (steps - turns * quarter) * (2.0 * math.pi / points)
    turns = turns - 4.0 * jnp.floor(turns * 0.25)
    square = angle * angle
    sine = jnp.full_like(square, 1.0 / 362880.0)
    for coefficient in (-1.0 / 5040.0, 1.0 / 120.0, -1.0 / 6.0, 1.0):
        sine = sine * square + coefficient
    sine = sine * angle
    cosine = jnp.full_like(square, 1.0 / 40320.0)
    for coefficient in (-1.0 / 720.0, 1.0 / 24.0, -0.5, 1.0):
        cosine = cosine * square + coefficient
    swap = (turns == 1.0) | (turns == 3.0)
    first = jnp.where(swap, sine, cosine)
    second = jnp.where(swap, cosine, sine)
    first = jnp.where((turns == 1.0) | (turns == 2.0), -first, first)
    second = jnp.where(turns >= 2.0, -second, second)
    return first, second


def fill_table(cols_ref, table_ref, points):
    devices, owned = cols_ref.shape
    factor = math.sqrt(2.0 / points)
    lane = iota((1, 128), 1).astype(F32)
    size = 64

    def body(chunk, carry):
        start = pl.multiple_of(chunk * size, size)
        waves = cols_ref[pl.ds(start, size), :].astype(F32)
        jump_cos, jump_sin = circle(waves * 128.0, points)
        for slot in range(owned):
            picked = slice(slot, slot + 1)
            cos0, sin0 = circle(waves[:, picked] * lane, points)
            cos0, sin0 = cos0 * factor, sin0 * factor
            turn_cos = jump_cos[:, picked] + jnp.zeros((1, 128), F32)
            turn_sin = jump_sin[:, picked] + jnp.zeros((1, 128), F32)
            cos1 = cos0 * turn_cos - sin0 * turn_sin
            sin1 = sin0 * turn_cos + cos0 * turn_sin
            twice = 2.0 * turn_cos
            rows = [pl.ds(pl.multiple_of((2 * slot + r) * devices + start, size), size) for r in range(2)]
            for index in range(points // 256):
                window = slice(128 * index, 128 * (index + 1))
                table_ref[rows[0], window] = cos0.astype(BF)
                table_ref[rows[1], window] = sin0.astype(BF)
                cos0, cos1 = cos1, twice * cos1 - cos0
                sin0, sin1 = sin1, twice * sin1 - sin0
        return carry

    lax.fori_loop(0, devices // size, body, 0)


def in_south(owner_ref, cols_ref):
    return (owner_ref[0] >= cols_ref.shape[0] // 2).astype(jnp.int32)


def grid_analysis(field, south, extra, cols_ref, table_ref, rhs_ref, stage_ref, send_ref):
    rows, points = field.shape
    devices, owned = cols_ref.shape
    rhs_ref[...] = make_rhs(field, south, rows, points // 2)
    signs = 1.0 - 2.0 * (cols_ref[...] & 1).astype(F32)
    lanes = iota((1, 128), 1)
    for place in range(SUB):
        acc = jnp.zeros((devices, 128), F32) + extra
        for group in range(GROUPS):
            slot = 2 * group + place // 2
            if slot < owned:
                first = (2 * slot + place % 2) * devices
                lines = project(table_ref[first : first + devices, :], rhs_ref[...], signs[:, slot : slot + 1])
                if group > 0:
                    lines = pltpu.roll(lines, group * rows, 1)
                acc = jnp.where((lanes >= group * rows) & (lanes < (group + 1) * rows), lines, acc)
        stage_ref[pl.ds(place, devices, stride=SUB), :] = acc
    send_ref[...] = stage_ref[...].astype(BF)


def grid_synthesis(received, south, cols_ref, table_ref, stage_ref, rows, points):
    devices, owned = cols_ref.shape
    source = iota((128, 128), 0)
    to = iota((128, 128), 1)
    base = jnp.where(to >= 2 * rows, 2 * rows, jnp.where(to >= rows, rows, 0))
    flipped = jnp.where((south > 0) & (to < SPARE), 2 * base + (rows - 1) - to, to)
    picker = jnp.where((source == flipped) & (to < SPARE), 1.0, 0.0).astype(BF)
    stage_ref[...] = mm(received, picker)
    signs = 1.0 - 2.0 * (cols_ref[...] & 1).astype(F32)
    signs = jnp.concatenate([signs, jnp.zeros((devices, 128 - owned), F32)], axis=1).T
    total = jnp.zeros((2 * rows, points // 2), F32)
    for place in range(SUB):
        across = stage_ref[pl.ds(place, devices, stride=SUB), :].T
        for group in range(GROUPS):
            slot = 2 * group + place // 2
            if slot < owned:
                lines = across[rows * group : rows * (group + 1)]
                lhs = jnp.concatenate([lines, lines * signs[slot : slot + 1]], axis=0).astype(BF)
                first = (2 * slot + place % 2) * devices
                total = total + mm(lhs, table_ref[first : first + devices, :])
    return jnp.concatenate([total[:rows], total[rows:]], axis=1)


def first_kernel(owner_ref, cols_ref, inn_hbm, mask_hbm, weight_hbm, basis_hbm,
                 table_ref, basis_ref, scale_ref, send_ref,
                 inn_ref, mask_ref, weight_ref, rhs_ref, stage_ref, sems):
    rows, points = inn_ref.shape
    pairs = ((inn_hbm, inn_ref), (mask_hbm, mask_ref), (weight_hbm, weight_ref), (basis_hbm, basis_ref))
    copies = [pltpu.make_async_copy(a, b, sems.at[i]) for i, (a, b) in enumerate(pairs)]
    for copy in copies:
        copy.start()
    fill_table(cols_ref, table_ref, points)
    for copy in copies[:3]:
        copy.wait()
    scale = mask_ref[...].astype(F32) * weight_ref[...]
    scale_ref[...] = scale
    grid_analysis(scale * inn_ref[...], in_south(owner_ref, cols_ref), jnp.zeros((1, 128), F32),
                  cols_ref, table_ref, rhs_ref, stage_ref, send_ref)
    copies[3].wait()


def middle_kernel(owner_ref, x_ref, table_ref, cols_ref, scale_ref,
                  field_ref, send_ref, scalar_ref, rhs_ref, stage_ref):
    rows, points = scale_ref.shape
    received = x_ref[...]
    (norm0,) = unpack_scalars(received.astype(F32), 1)
    field = grid_synthesis(received, in_south(owner_ref, cols_ref), cols_ref, table_ref, stage_ref, rows, points)
    field_ref[...] = field
    scaled = scale_ref[...] * field
    energy = jnp.sum(scaled * field)
    scalar_ref[...] = jnp.zeros((8, 128), F32) + norm0
    grid_analysis(scaled, in_south(owner_ref, cols_ref), pack_scalars([norm0, energy]),
                  cols_ref, table_ref, rhs_ref, stage_ref, send_ref)


def last_kernel(owner_ref, x_ref, table_ref, cols_ref, scale_ref, first_ref, scalar_in,
                field_ref, energy_ref, scalar_ref, stage_ref):
    rows, points = scale_ref.shape
    received = x_ref[...]
    norm1, cross = unpack_scalars(received.astype(F32), 2)
    norm0 = scalar_in[0:1, 0:1]
    beta = (jnp.zeros((1, 1), F32) + norm1) / norm0
    field = grid_synthesis(received, in_south(owner_ref, cols_ref), cols_ref, table_ref, stage_ref, rows, points)
    field = field + beta * first_ref[...]
    field_ref[...] = field
    energy_ref[...] = jnp.zeros(energy_ref.shape, F32) + jnp.sum(scale_ref[...] * field * field)
    line = iota((8, 128), 0)
    scalar_ref[...] = jnp.where(line == 0, norm1, cross)


def lane_windows(band, rows):
    start = band * rows
    block, offset = start // 128, start % 128
    if offset + rows <= 128:
        return [(block, offset, offset + rows)]
    return [(block, offset, 128), (block + 1, 0, offset + rows - 128)]


def chooser(part, transposed):
    shape = (64, 32) if transposed else (32, 64)
    fine = iota(shape, 1 if transposed else 0)
    wide = iota(shape, 0 if transposed else 1)
    where = (fine >> 4) * 32 + (fine & 7) * SUB + 2 * part + ((fine >> 3) & 1)
    return jnp.where(wide == where, 1.0, 0.0).astype(BF)


def parity_row(wave, degrees):
    offset = iota((1, degrees), 1) - wave
    return jnp.where(offset >= 0, 1.0 - 2.0 * (offset & 1).astype(F32), 0.0)


def spectral_kernel(rows, with_base, owner_ref, order_ref, x_ref, basis_ref, spread_ref, *refs):
    if with_base:
        base_ref, out_ref, send_ref, scalar_ref = refs
    else:
        out_ref, send_ref, scalar_ref = refs
    owned, half_rows, degrees = basis_ref.shape
    bands = half_rows // rows
    received = x_ref[...].astype(F32)
    lane = iota((1, 128), 1)
    if with_base:
        norm0, energy = unpack_scalars(received, 2)
        norm0 = (jnp.zeros((1, 1), F32) + norm0) * (1.0 / (2 * bands * 8))
        step_size = norm0 / (norm0 + energy)
        scalar_ref[...] = jnp.zeros((8, 128), F32) + step_size
    spread_rows = jnp.concatenate([spread_ref[...], spread_ref[...]], axis=0)
    blocks = half_rows // 128
    lines = []
    for group in range(GROUPS):
        parts = []
        for side in range(2):
            columns = [jnp.zeros((32, 128), F32)] * blocks
            for band in range(bands):
                row = band if side == 0 else 2 * bands - 1 - band
                block = received[32 * row : 32 * row + 32]
                shift = (rows * band - rows * group) % 128
                if shift:
                    block = pltpu.roll(block, shift, 1)
                for index, low, high in lane_windows(band, rows):
                    columns[index] = jnp.where((lane >= low) & (lane < high), block, columns[index])
            parts.append(jnp.concatenate(columns, axis=1))
        lines.append(jnp.concatenate(parts, axis=0).astype(BF))
    norm = jnp.zeros((1, 1), F32)
    cross = jnp.zeros((1, 1), F32)
    parities = []
    for slot in range(owned):
        parity = parity_row(order_ref[owner_ref[0] * owned + slot], degrees)
        parities.append(parity)
        lhs = mm(chooser(slot % 2, False), lines[slot // 2]).astype(BF)
        sums = mm(lhs, basis_ref[slot])
        value = (sums[:16] * jnp.abs(parity) + parity * sums[16:]) * spread_rows
        if with_base:
            base = base_ref[slot]
            value = base - step_size * (base + value)
            cross = cross + jnp.sum(value * base)
        out_ref[slot] = value
        norm = norm + jnp.sum(value * value)
    if with_base:
        extra = pack_scalars([norm, cross])
    else:
        extra = pack_scalars([norm])
        scalar_ref[...] = jnp.zeros((8, 128), F32)
    wide = [None] * GROUPS
    for slot in range(owned):
        parity = parities[slot]
        coeff = (out_ref[slot] * spread_rows * jnp.abs(parity)).astype(BF).astype(F32)
        even = jnp.where(parity > 0, coeff, 0.0)
        odd = jnp.where(parity < 0, coeff, 0.0)
        sums = mm_nt(jnp.concatenate([even, odd], axis=0).astype(BF), basis_ref[slot])
        sides = jnp.concatenate([sums[:16] + sums[16:], sums[:16] - sums[16:]], axis=0).astype(BF)
        spreaded = mm(chooser(slot % 2, True), sides)
        group = slot // 2
        wide[group] = spreaded if wide[group] is None else wide[group] + spreaded
    for side in range(2):
        for band in range(bands):
            block = jnp.zeros((32, 128), F32) + extra
            for group in range(GROUPS):
                shift = (rows * group - rows * band) % 128
                place = rows * group
                for index, low, high in lane_windows(band, rows):
                    source = wide[group][32 * side : 32 * side + 32, 128 * index : 128 * index + 128]
                    if shift:
                        source = pltpu.roll(source, shift, 1)
                    block = jnp.where((lane >= place) & (lane < place + high - low), source, block)
                    place += high - low
            row = band if side == 0 else 2 * bands - 1 - band
            send_ref[32 * row : 32 * row + 32, :] = block.astype(BF)


def finish_kernel(energy_ref, norm0_ref, norms_ref, step_ref, rhs_ref, residual_ref, field1_ref, field2_ref,
                  control_ref, increment_ref):
    total = jnp.sum(energy_ref[...], axis=0, keepdims=True)[:, 0:1]
    first = norm0_ref[0:1, 0:1]
    norm1 = norms_ref[0:1, 0:1]
    cross = norms_ref[1:2, 0:1]
    step1 = step_ref[0:1, 0:1]
    beta = norm1 / first
    step2 = norm1 / (norm1 + 2.0 * beta * cross + beta * beta * first + total)
    mixed = step1 + step2 * beta
    for slot in range(rhs_ref.shape[0]):
        control_ref[slot] = mixed * rhs_ref[slot] + step2 * residual_ref[slot]
    increment_ref[...] = step1 * field1_ref[...] + step2 * field2_ref[...]


SMEM = pl.BlockSpec(memory_space=pltpu.SMEM)
VMEM = pl.BlockSpec(memory_space=pltpu.VMEM)
HBM = pl.BlockSpec(memory_space=pltpu.HBM)


def near(array):
    return pltpu.with_memory_space_constraint(array, pltpu.VMEM)


def far(array):
    return pltpu.with_memory_space_constraint(array, pltpu.HBM)


def shape(dims, dtype):
    return jax.ShapeDtypeStruct(dims, dtype)


def exchange(buffer):
    return lax.all_to_all(buffer, ("lat", "lev"), split_axis=0, concat_axis=0, tiled=True)


def local(innovation, obs_mask, obs_weight, order, basis, spread):
    lat = lax.axis_index("lat")
    lev = lax.axis_index("lev")
    devices = lax.axis_size("lat") * lax.axis_size("lev")
    owned, half_rows, degrees = basis.shape
    rows, points = innovation.shape[1:]
    half = points // 2
    chunk_rows = devices * SUB
    owner = (lat * lax.axis_size("lev") + lev).astype(jnp.int32).reshape(1)
    cols = order.reshape(devices, owned)
    table_rows = 2 * owned * devices
    stage = pltpu.VMEM((chunk_rows, 128), F32)
    rhs_part = pltpu.VMEM((256, half), BF)
    plane = (rows, points)

    table, basis, scale, send = pl.pallas_call(
        first_kernel,
        in_specs=[SMEM, VMEM, HBM, HBM, HBM, HBM],
        out_specs=[VMEM] * 4,
        out_shape=[
            pltpu.VMEM((table_rows, half), BF),
            pltpu.VMEM(basis.shape, BF),
            pltpu.VMEM(plane, F32),
            shape((chunk_rows, 128), BF),
        ],
        scratch_shapes=[pltpu.VMEM(plane, F32), pltpu.VMEM(plane, jnp.int32), pltpu.VMEM(plane, F32)]
        + [rhs_part, stage, pltpu.SemaphoreType.DMA((4,))],
        compiler_params=params(),
        name="first",
    )(owner, cols, *map(far, (innovation.reshape(plane), obs_mask.reshape(plane), obs_weight.reshape(plane), basis)))
    table, basis, scale = map(near, (table, basis, scale))

    def spectral(received, base):
        with_base = base is not None
        return pl.pallas_call(
            functools.partial(spectral_kernel, rows, with_base),
            in_specs=[SMEM, SMEM, VMEM, VMEM, VMEM] + [VMEM] * with_base,
            out_specs=[VMEM] * 3,
            out_shape=[shape((owned, 16, degrees), F32), shape((chunk_rows, 128), BF), shape((8, 128), F32)],
            compiler_params=params(),
            name="spectral",
        )(owner, order, received, basis, spread, *([base] * with_base))

    rhs, send, _ = spectral(exchange(send), None)
    field1, send, norm0 = pl.pallas_call(
        middle_kernel,
        in_specs=[SMEM, VMEM, VMEM, VMEM, VMEM],
        out_specs=[VMEM] * 3,
        out_shape=[shape(plane, F32), shape((chunk_rows, 128), BF), shape((8, 128), F32)],
        scratch_shapes=[rhs_part, stage],
        compiler_params=params(),
        name="middle",
    )(owner, exchange(send), table, cols, scale)
    residual, send, step1 = spectral(exchange(send), rhs)
    field2, energy, norms = pl.pallas_call(
        last_kernel,
        in_specs=[SMEM] + [VMEM] * 6,
        out_specs=[VMEM] * 3,
        out_shape=[shape(plane, F32), shape((devices, 128), F32), shape((8, 128), F32)],
        scratch_shapes=[stage],
        compiler_params=params(),
        name="last",
    )(owner, exchange(send), table, cols, scale, field1, norm0)
    control, increment = pl.pallas_call(
        finish_kernel,
        in_specs=[VMEM] * 8,
        out_specs=[VMEM] * 2,
        out_shape=[shape(rhs.shape, F32), shape(plane, F32)],
        compiler_params=params(),
        name="finish",
    )(exchange(energy), norm0, norms, step1, rhs, residual, field1, field2)
    return (control, increment.reshape(innovation.shape))


def solution(mesh):
    in_specs = (
        P("lev", "lat", None),
        P("lev", "lat", None),
        P("lev", "lat", None),
        P(),
        P(("lat", "lev"), None, None),
        P(),
    )
    out_specs = (P(("lat", "lev"), None, None), P("lev", "lat", None))
    return jax.shard_map(local, mesh=mesh, in_specs=in_specs, out_specs=out_specs, check_vma=False)
```

```python
import functools
import math

import jax
import jax.numpy as jnp
from jax import lax
from jax.experimental import pallas as pl
from jax.experimental.pallas import tpu as pltpu
from jax.sharding import PartitionSpec as P

BF = jnp.bfloat16
F32 = jnp.float32
GROUPS = 3
SUB = 4
SPARE = 120
VMEM_LIMIT = 20 * 1024 * 1024


def iota(shape, axis):
    return lax.broadcasted_iota(jnp.int32, shape, axis)


def params():
    return pltpu.CompilerParams(vmem_limit_bytes=VMEM_LIMIT)


def mm(a, b):
    return jnp.dot(a, b, preferred_element_type=F32)


def mm_nt(a, b):
    return lax.dot_general(a, b, (((1,), (1,)), ((), ())), preferred_element_type=F32)


def pack_scalars(values):
    lane = iota((1, 128), 1)
    out = jnp.zeros((1, 128), F32)
    for index, value in enumerate(values):
        rest = jnp.zeros((1, 128), F32) + value
        for piece in range(3):
            part = rest.astype(BF).astype(F32)
            rest = rest - part
            out = jnp.where(lane == SPARE + 3 * index + piece, part, out)
    return out


def unpack_scalars(received, count):
    total = jnp.sum(received, axis=0, keepdims=True) * (1.0 / SUB)
    lane = iota((1, 128), 1)
    sums = []
    for index in range(count):
        first = SPARE + 3 * index
        sums.append(jnp.sum(jnp.where((lane >= first) & (lane < first + 3), total, 0.0)))
    return sums


def reverse_lanes(pieces):
    width = pieces.shape[1]
    flip = jnp.where(iota((128, 128), 0) + iota((128, 128), 1) == 127, 1.0, 0.0).astype(BF)
    return jnp.concatenate([mm(pieces[:, first : first + 128], flip) for first in range(width - 128, -1, -128)], axis=1)


def split(values, count):
    pieces = []
    for _ in range(count):
        pieces.append(values.astype(BF).astype(F32))
        values = values - pieces[-1]
    return pieces


def make_rhs(field, south):
    rows, points = field.shape
    width = points // 4
    quarters = [field[:, width * i : width * (i + 1)] for i in range(4)]
    pieces = split(quarters[1], 2) + split(quarters[3], 2)
    back = reverse_lanes(jnp.concatenate(pieces, axis=0).astype(BF))
    back1 = back[:rows] + back[rows : 2 * rows]
    back3 = back[2 * rows : 3 * rows] + back[3 * rows :]
    gap = jnp.zeros((64 - rows, width), F32)

    def bands(plain, signed):
        parts = []
        for piece in split(plain, 2) + split(signed, 2):
            parts += [piece, gap]
        return jnp.concatenate(parts, axis=0)

    stacked = jnp.concatenate(
        [bands(quarters[0] + back3, quarters[2] + back1), bands(quarters[0] - back3, quarters[2] - back1)], axis=1
    ).astype(BF)
    to = iota((256, 256), 0)
    source = iota((256, 256), 1)
    inner = to & 63
    flipped = jnp.where((south > 0) & (inner < rows), to - inner + (rows - 1) - inner, to)
    picker = jnp.where(source == flipped, 1.0, 0.0).astype(BF)
    return mm(picker, stacked).astype(BF)


def project(table, rhs, sign):
    product = mm_nt(table, rhs)
    both = product[:, :128] + sign * product[:, 128:]
    return both + pltpu.roll(both, 64, 1)


def circle(steps, points):
    quarter = points // 4
    turns = jnp.floor(steps * (1.0 / quarter) + 0.5)
    angle = (steps - turns * quarter) * (2.0 * math.pi / points)
    turns = turns - 4.0 * jnp.floor(turns * 0.25)
    square = angle * angle
    sine = jnp.full_like(square, 1.0 / 362880.0)
    for coefficient in (-1.0 / 5040.0, 1.0 / 120.0, -1.0 / 6.0, 1.0):
        sine = sine * square + coefficient
    sine = sine * angle
    cosine = jnp.full_like(square, 1.0 / 40320.0)
    for coefficient in (-1.0 / 720.0, 1.0 / 24.0, -0.5, 1.0):
        cosine = cosine * square + coefficient
    swap = (turns == 1.0) | (turns == 3.0)
    first = jnp.where(swap, sine, cosine)
    second = jnp.where(swap, cosine, sine)
    first = jnp.where((turns == 1.0) | (turns == 2.0), -first, first)
    second = jnp.where(turns >= 2.0, -second, second)
    return first, second


def fill_table(cols_ref, table_ref, turn_ref, points):
    devices, owned = cols_ref.shape
    factor = math.sqrt(2.0 / points)
    lane = iota((1, 128), 1).astype(F32)
    size = 64

    def body(chunk, carry):
        start = pl.multiple_of(chunk * size, size)
        whole = cols_ref[pl.ds(start, size), :]
        waves = whole.astype(F32)
        half_cos, half_sin = circle(waves, 2 * points)
        sign = 1.0 - 2.0 * (whole & 1).astype(F32)
        gap = jnp.zeros((size, 8 - owned), F32)
        rest = jnp.zeros((size, 128 - 24), F32)
        turn_ref[pl.ds(start, size), :] = jnp.concatenate([half_cos, gap, half_sin, gap, sign, gap, rest], axis=1)
        jump_cos, jump_sin = circle(waves * 256.0, 2 * points)
        for slot in range(owned):
            picked = slice(slot, slot + 1)
            cos0, sin0 = circle(waves[:, picked] * (2.0 * lane + 1.0), 2 * points)
            cos0, sin0 = cos0 * factor, sin0 * factor
            turn_cos = jump_cos[:, picked] + jnp.zeros((1, 128), F32)
            turn_sin = jump_sin[:, picked] + jnp.zeros((1, 128), F32)
            cos1 = cos0 * turn_cos - sin0 * turn_sin
            sin1 = sin0 * turn_cos + cos0 * turn_sin
            twice = 2.0 * turn_cos
            rows = [pl.ds(pl.multiple_of((2 * slot + r) * devices + start, size), size) for r in range(2)]
            for index in range(points // 512):
                window = slice(128 * index, 128 * (index + 1))
                table_ref[rows[0], window] = cos0.astype(BF)
                table_ref[rows[1], window] = sin0.astype(BF)
                cos0, cos1 = cos1, twice * cos1 - cos0
                sin0, sin1 = sin1, twice * sin1 - sin0
        return carry

    lax.fori_loop(0, devices // size, body, 0)


def in_south(owner_ref, turn_ref):
    return (owner_ref[0] >= turn_ref.shape[0] // 2).astype(jnp.int32)


def grid_analysis(field, south, extra, turn_ref, table_ref, rhs_ref, stage_ref, send_ref):
    rows, points = field.shape
    devices = turn_ref.shape[0]
    owned = table_ref.shape[0] // (2 * devices)
    width = points // 4
    rhs_ref[...] = make_rhs(field, south)
    turns = turn_ref[...]
    lanes = iota((1, 128), 1)
    parts = [jnp.zeros((devices, 128), F32) + extra] * SUB
    for slot in range(owned):
        group = slot // 2
        mine = (lanes >= group * rows) & (lanes < (group + 1) * rows)
        sign = turns[:, 16 + slot : 17 + slot]
        sums = []
        for r in range(2):
            first = (2 * slot + r) * devices
            sums.append(project(table_ref[first : first + devices, :], rhs_ref[:, width * r : width * (r + 1)], sign))
        half_cos = turns[:, slot : slot + 1]
        half_sin = turns[:, 8 + slot : 9 + slot]
        turned = [sums[0] * half_cos + sums[1] * half_sin, sums[1] * half_cos - sums[0] * half_sin]
        for r in range(2):
            lines = pltpu.roll(turned[r], group * rows, 1) if group > 0 else turned[r]
            place = 2 * (slot % 2) + r
            parts[place] = jnp.where(mine, lines, parts[place])
    for place in range(SUB):
        stage_ref[pl.ds(place, devices, stride=SUB), :] = parts[place]
    send_ref[...] = stage_ref[...].astype(BF)


def grid_synthesis(received, south, turn_ref, table_ref, stage_ref, rows):
    devices = turn_ref.shape[0]
    owned = table_ref.shape[0] // (2 * devices)
    width = table_ref.shape[1]
    source = iota((128, 128), 0)
    to = iota((128, 128), 1)
    base = jnp.where(to >= 2 * rows, 2 * rows, jnp.where(to >= rows, rows, 0))
    flipped = jnp.where((south > 0) & (to < SPARE), 2 * base + (rows - 1) - to, to)
    picker = jnp.where((source == flipped) & (to < SPARE), 1.0, 0.0).astype(BF)
    stage_ref[...] = mm(received, picker)
    turns = turn_ref[...].T
    totals = [jnp.zeros((2 * rows, width), F32)] * 2
    for part in range(2):
        across = [stage_ref[pl.ds(2 * part + r, devices, stride=SUB), :].T for r in range(2)]
        for group in range(GROUPS):
            slot = 2 * group + part
            if slot < owned:
                cosines, sines = [lines[rows * group : rows * (group + 1)] for lines in across]
                half_cos = turns[slot : slot + 1]
                half_sin = turns[8 + slot : 9 + slot]
                sign = turns[16 + slot : 17 + slot]
                turned = [cosines * half_cos - sines * half_sin, cosines * half_sin + sines * half_cos]
                for r in range(2):
                    lhs = jnp.concatenate([turned[r], turned[r] * sign], axis=0).astype(BF)
                    first = (2 * slot + r) * devices
                    totals[r] = totals[r] + mm(lhs, table_ref[first : first + devices, :])
    ahead = totals[0] + totals[1]
    count = 2 * rows
    back = reverse_lanes(jnp.concatenate(split(totals[0] - totals[1], 3), axis=0).astype(BF))
    back = back[:count] + back[count : 2 * count] + back[2 * count :]
    return jnp.concatenate([ahead[:rows], back[rows:], ahead[rows:], back[:rows]], axis=1)


def first_kernel(owner_ref, cols_ref, inn_hbm, mask_hbm, weight_hbm, basis_hbm,
                 table_ref, turn_ref, basis_ref, scale_ref, send_ref,
                 inn_ref, mask_ref, weight_ref, rhs_ref, stage_ref, sems):
    points = inn_ref.shape[1]
    pairs = ((inn_hbm, inn_ref), (mask_hbm, mask_ref), (weight_hbm, weight_ref), (basis_hbm, basis_ref))
    copies = [pltpu.make_async_copy(a, b, sems.at[i]) for i, (a, b) in enumerate(pairs)]
    for copy in copies:
        copy.start()
    fill_table(cols_ref, table_ref, turn_ref, points)
    for copy in copies[:3]:
        copy.wait()
    scale = mask_ref[...].astype(F32) * weight_ref[...]
    scale_ref[...] = scale
    grid_analysis(scale * inn_ref[...], in_south(owner_ref, turn_ref), jnp.zeros((1, 128), F32),
                  turn_ref, table_ref, rhs_ref, stage_ref, send_ref)
    copies[3].wait()


def middle_kernel(owner_ref, x_ref, table_ref, turn_ref, scale_ref,
                  field_ref, send_ref, scalar_ref, rhs_ref, stage_ref):
    rows = scale_ref.shape[0]
    south = in_south(owner_ref, turn_ref)
    received = x_ref[...]
    (norm0,) = unpack_scalars(received.astype(F32), 1)
    field = grid_synthesis(received, south, turn_ref, table_ref, stage_ref, rows)
    field_ref[...] = field
    scaled = scale_ref[...] * field
    energy = jnp.sum(scaled * field)
    scalar_ref[...] = jnp.zeros((8, 128), F32) + norm0
    grid_analysis(scaled, south, pack_scalars([norm0, energy]), turn_ref, table_ref, rhs_ref, stage_ref, send_ref)


def last_kernel(owner_ref, x_ref, table_ref, turn_ref, scale_ref, first_ref, scalar_in,
                field_ref, energy_ref, scalar_ref, stage_ref):
    rows = scale_ref.shape[0]
    received = x_ref[...]
    norm1, cross = unpack_scalars(received.astype(F32), 2)
    norm0 = scalar_in[0:1, 0:1]
    beta = (jnp.zeros((1, 1), F32) + norm1) / norm0
    field = grid_synthesis(received, in_south(owner_ref, turn_ref), turn_ref, table_ref, stage_ref, rows)
    field = field + beta * first_ref[...]
    field_ref[...] = field
    energy_ref[...] = jnp.zeros(energy_ref.shape, F32) + jnp.sum(scale_ref[...] * field * field)
    line = iota((8, 128), 0)
    scalar_ref[...] = jnp.where(line == 0, norm1, cross)


def lane_windows(band, rows):
    start = band * rows
    block, offset = start // 128, start % 128
    if offset + rows <= 128:
        return [(block, offset, offset + rows)]
    return [(block, offset, 128), (block + 1, 0, offset + rows - 128)]


def chooser(part, transposed):
    shape = (64, 32) if transposed else (32, 64)
    fine = iota(shape, 1 if transposed else 0)
    wide = iota(shape, 0 if transposed else 1)
    where = (fine >> 4) * 32 + (fine & 7) * SUB + 2 * part + ((fine >> 3) & 1)
    return jnp.where(wide == where, 1.0, 0.0).astype(BF)


def parity_row(wave, degrees):
    offset = iota((1, degrees), 1) - wave
    return jnp.where(offset >= 0, 1.0 - 2.0 * (offset & 1).astype(F32), 0.0)


def spectral_kernel(rows, with_base, owner_ref, order_ref, x_ref, basis_ref, spread_ref, *refs):
    if with_base:
        base_ref, out_ref, send_ref, scalar_ref = refs
    else:
        out_ref, send_ref = refs
    owned, half_rows, degrees = basis_ref.shape
    bands = half_rows // rows
    received = x_ref[...].astype(F32)
    lane = iota((1, 128), 1)
    if with_base:
        norm0, energy = unpack_scalars(received, 2)
        norm0 = (jnp.zeros((1, 1), F32) + norm0) * (1.0 / (2 * bands * 8))
        step_size = norm0 / (norm0 + energy)
        scalar_ref[...] = jnp.zeros((8, 128), F32) + step_size
    spread_rows = jnp.concatenate([spread_ref[...], spread_ref[...]], axis=0)
    blocks = half_rows // 128
    lines = []
    for group in range(GROUPS):
        parts = []
        for side in range(2):
            columns = [jnp.zeros((32, 128), F32)] * blocks
            for band in range(bands):
                row = band if side == 0 else 2 * bands - 1 - band
                block = received[32 * row : 32 * row + 32]
                shift = (rows * band - rows * group) % 128
                if shift:
                    block = pltpu.roll(block, shift, 1)
                for index, low, high in lane_windows(band, rows):
                    columns[index] = jnp.where((lane >= low) & (lane < high), block, columns[index])
            parts.append(jnp.concatenate(columns, axis=1))
        lines.append(jnp.concatenate(parts, axis=0).astype(BF))
    norm = jnp.zeros((16, degrees), F32)
    cross = jnp.zeros((16, degrees), F32)
    parities = []
    for slot in range(owned):
        parity = parity_row(order_ref[owner_ref[0] * owned + slot], degrees)
        parities.append(parity)
        lhs = mm(chooser(slot % 2, False), lines[slot // 2]).astype(BF)
        sums = mm(lhs, basis_ref[slot])
        value = (sums[:16] * jnp.abs(parity) + parity * sums[16:]) * spread_rows
        if with_base:
            base = base_ref[slot]
            value = base - step_size * (base + value)
            cross = cross + value * base
        out_ref[slot] = value
        norm = norm + value * value
    if with_base:
        extra = pack_scalars([jnp.sum(norm), jnp.sum(cross)])
    else:
        extra = pack_scalars([jnp.sum(norm)])
    wide = [None] * GROUPS
    for slot in range(owned):
        parity = parities[slot]
        coeff = (out_ref[slot] * spread_rows * jnp.abs(parity)).astype(BF).astype(F32)
        even = jnp.where(parity > 0, coeff, 0.0)
        odd = jnp.where(parity < 0, coeff, 0.0)
        sums = mm_nt(jnp.concatenate([even, odd], axis=0).astype(BF), basis_ref[slot])
        sides = jnp.concatenate([sums[:16] + sums[16:], sums[:16] - sums[16:]], axis=0).astype(BF)
        spreaded = mm(chooser(slot % 2, True), sides)
        group = slot // 2
        wide[group] = spreaded if wide[group] is None else wide[group] + spreaded
    for side in range(2):
        for band in range(bands):
            block = jnp.zeros((32, 128), F32) + extra
            for group in range(GROUPS):
                shift = (rows * group - rows * band) % 128
                place = rows * group
                for index, low, high in lane_windows(band, rows):
                    source = wide[group][32 * side : 32 * side + 32, 128 * index : 128 * index + 128]
                    if shift:
                        source = pltpu.roll(source, shift, 1)
                    block = jnp.where((lane >= place) & (lane < place + high - low), source, block)
                    place += high - low
            row = band if side == 0 else 2 * bands - 1 - band
            send_ref[32 * row : 32 * row + 32, :] = block.astype(BF)


def finish_kernel(energy_ref, norm0_ref, norms_ref, step_ref, rhs_ref, residual_ref, field1_ref, field2_ref,
                  control_ref, increment_ref):
    total = jnp.sum(energy_ref[...], axis=0, keepdims=True)[:, 0:1]
    first = norm0_ref[0:1, 0:1]
    norm1 = norms_ref[0:1, 0:1]
    cross = norms_ref[1:2, 0:1]
    step1 = step_ref[0:1, 0:1]
    beta = norm1 / first
    step2 = norm1 / (norm1 + 2.0 * beta * cross + beta * beta * first + total)
    mixed = step1 + step2 * beta
    for slot in range(rhs_ref.shape[0]):
        control_ref[slot] = mixed * rhs_ref[slot] + step2 * residual_ref[slot]
    increment_ref[...] = step1 * field1_ref[...] + step2 * field2_ref[...]


SMEM = pl.BlockSpec(memory_space=pltpu.SMEM)
VMEM = pl.BlockSpec(memory_space=pltpu.VMEM)
HBM = pl.BlockSpec(memory_space=pltpu.HBM)


def near(array):
    return pltpu.with_memory_space_constraint(array, pltpu.VMEM)


def far(array):
    return pltpu.with_memory_space_constraint(array, pltpu.HBM)


def shape(dims, dtype):
    return jax.ShapeDtypeStruct(dims, dtype)


def exchange(buffer):
    return lax.all_to_all(buffer, ("lat", "lev"), split_axis=0, concat_axis=0, tiled=True)


def local(innovation, obs_mask, obs_weight, order, basis, spread):
    lat = lax.axis_index("lat")
    lev = lax.axis_index("lev")
    devices = lax.axis_size("lat") * lax.axis_size("lev")
    owned, half_rows, degrees = basis.shape
    rows, points = innovation.shape[1:]
    chunk_rows = devices * SUB
    owner = (lat * lax.axis_size("lev") + lev).astype(jnp.int32).reshape(1)
    cols = order.reshape(devices, owned)
    table_rows = 2 * owned * devices
    stage = pltpu.VMEM((chunk_rows, 128), F32)
    rhs_part = pltpu.VMEM((256, points // 2), BF)
    plane = (rows, points)

    table, turn, basis, scale, send = pl.pallas_call(
        first_kernel,
        in_specs=[SMEM, VMEM, HBM, HBM, HBM, HBM],
        out_specs=[VMEM] * 5,
        out_shape=[
            pltpu.VMEM((table_rows, points // 4), BF),
            pltpu.VMEM((devices, 128), F32),
            pltpu.VMEM(basis.shape, BF),
            pltpu.VMEM(plane, F32),
            shape((chunk_rows, 128), BF),
        ],
        scratch_shapes=[pltpu.VMEM(plane, F32), pltpu.VMEM(plane, jnp.int32), pltpu.VMEM(plane, F32)]
        + [rhs_part, stage, pltpu.SemaphoreType.DMA((4,))],
        compiler_params=params(),
        name="first",
    )(owner, cols, *map(far, (innovation.reshape(plane), obs_mask.reshape(plane), obs_weight.reshape(plane), basis)))
    table, turn, basis, scale = map(near, (table, turn, basis, scale))

    def spectral(received, base):
        with_base = base is not None
        return pl.pallas_call(
            functools.partial(spectral_kernel, rows, with_base),
            in_specs=[SMEM, SMEM, VMEM, VMEM, VMEM] + [VMEM] * with_base,
            out_specs=[VMEM] * (2 + with_base),
            out_shape=[shape((owned, 16, degrees), F32), shape((chunk_rows, 128), BF)]
            + [shape((8, 128), F32)] * with_base,
            compiler_params=params(),
            name="spectral",
        )(owner, order, received, basis, spread, *([base] * with_base))

    rhs, send = spectral(exchange(send), None)
    field1, send, norm0 = pl.pallas_call(
        middle_kernel,
        in_specs=[SMEM, VMEM, VMEM, VMEM, VMEM],
        out_specs=[VMEM] * 3,
        out_shape=[shape(plane, F32), shape((chunk_rows, 128), BF), shape((8, 128), F32)],
        scratch_shapes=[rhs_part, stage],
        compiler_params=params(),
        name="middle",
    )(owner, exchange(send), table, turn, scale)
    residual, send, step1 = spectral(exchange(send), rhs)
    field2, energy, norms = pl.pallas_call(
        last_kernel,
        in_specs=[SMEM] + [VMEM] * 6,
        out_specs=[VMEM] * 3,
        out_shape=[shape(plane, F32), shape((devices, 128), F32), shape((8, 128), F32)],
        scratch_shapes=[stage],
        compiler_params=params(),
        name="last",
    )(owner, exchange(send), table, turn, scale, field1, norm0)
    control, increment = pl.pallas_call(
        finish_kernel,
        in_specs=[VMEM] * 8,
        out_specs=[VMEM] * 2,
        out_shape=[shape(rhs.shape, F32), shape(plane, F32)],
        compiler_params=params(),
        name="finish",
    )(exchange(energy), norm0, norms, step1, rhs, residual, field1, field2)
    return (control, increment.reshape(innovation.shape))


def solution(mesh):
    in_specs = (
        P("lev", "lat", None),
        P("lev", "lat", None),
        P("lev", "lat", None),
        P(),
        P(("lat", "lev"), None, None),
        P(),
    )
    out_specs = (P(("lat", "lev"), None, None), P("lev", "lat", None))
    return jax.shard_map(local, mesh=mesh, in_specs=in_specs, out_specs=out_specs, check_vma=False)
```

```python
import functools
import math

import jax
import jax.numpy as jnp
from jax import lax
from jax.experimental import pallas as pl
from jax.experimental.pallas import tpu as pltpu
from jax.sharding import PartitionSpec as P

BF = jnp.bfloat16
F32 = jnp.float32
GROUPS = 3
SUB = 4
SPARE = 120
VMEM_LIMIT = 20 * 1024 * 1024


def iota(shape, axis):
    return lax.broadcasted_iota(jnp.int32, shape, axis)


def params():
    return pltpu.CompilerParams(vmem_limit_bytes=VMEM_LIMIT)


def mm(a, b):
    return jnp.dot(a, b, preferred_element_type=F32)


def mm_nt(a, b):
    return lax.dot_general(a, b, (((1,), (1,)), ((), ())), preferred_element_type=F32)


def pack_scalars(values):
    lane = iota((1, 128), 1)
    out = jnp.zeros((1, 128), F32)
    for index, value in enumerate(values):
        rest = jnp.zeros((1, 128), F32) + value
        for piece in range(3):
            part = rest.astype(BF).astype(F32)
            rest = rest - part
            out = jnp.where(lane == SPARE + 3 * index + piece, part, out)
    return out


def unpack_scalars(received, count):
    total = jnp.sum(received, axis=0, keepdims=True) * (1.0 / SUB)
    lane = iota((1, 128), 1)
    sums = []
    for index in range(count):
        first = SPARE + 3 * index
        sums.append(jnp.sum(jnp.where((lane >= first) & (lane < first + 3), total, 0.0)))
    return sums


def reverse_lanes(pieces):
    width = pieces.shape[1]
    flip = jnp.where(iota((128, 128), 0) + iota((128, 128), 1) == 127, 1.0, 0.0).astype(BF)
    return jnp.concatenate([mm(pieces[:, first : first + 128], flip) for first in range(width - 128, -1, -128)], axis=1)


def split(values, count):
    pieces = []
    for _ in range(count):
        pieces.append(values.astype(BF).astype(F32))
        values = values - pieces[-1]
    return pieces


def make_rhs(field, south):
    rows, points = field.shape
    width = points // 4
    quarters = [field[:, width * i : width * (i + 1)] for i in range(4)]
    pieces = split(quarters[1], 2) + split(quarters[3], 2)
    back = reverse_lanes(jnp.concatenate(pieces, axis=0).astype(BF))
    back1 = back[:rows] + back[rows : 2 * rows]
    back3 = back[2 * rows : 3 * rows] + back[3 * rows :]
    gap = jnp.zeros((64 - rows, width), F32)

    def bands(plain, signed):
        parts = []
        for piece in split(plain, 2) + split(signed, 2):
            parts += [piece, gap]
        return jnp.concatenate(parts, axis=0)

    stacked = jnp.concatenate(
        [bands(quarters[0] + back3, quarters[2] + back1), bands(quarters[0] - back3, quarters[2] - back1)], axis=1
    ).astype(BF)
    to = iota((256, 256), 0)
    source = iota((256, 256), 1)
    inner = to & 63
    flipped = jnp.where((south > 0) & (inner < rows), to - inner + (rows - 1) - inner, to)
    picker = jnp.where(source == flipped, 1.0, 0.0).astype(BF)
    return mm(picker, stacked).astype(BF)


def project(table, rhs, sign):
    product = mm_nt(table, rhs)
    both = product[:, :128] + sign * product[:, 128:]
    return both + pltpu.roll(both, 64, 1)


def circle(steps, points):
    quarter = points // 4
    turns = jnp.floor(steps * (1.0 / quarter) + 0.5)
    angle = (steps - turns * quarter) * (2.0 * math.pi / points)
    turns = turns - 4.0 * jnp.floor(turns * 0.25)
    square = angle * angle
    sine = jnp.full_like(square, 1.0 / 362880.0)
    for coefficient in (-1.0 / 5040.0, 1.0 / 120.0, -1.0 / 6.0, 1.0):
        sine = sine * square + coefficient
    sine = sine * angle
    cosine = jnp.full_like(square, 1.0 / 40320.0)
    for coefficient in (-1.0 / 720.0, 1.0 / 24.0, -0.5, 1.0):
        cosine = cosine * square + coefficient
    swap = (turns == 1.0) | (turns == 3.0)
    first = jnp.where(swap, sine, cosine)
    second = jnp.where(swap, cosine, sine)
    first = jnp.where((turns == 1.0) | (turns == 2.0), -first, first)
    second = jnp.where(turns >= 2.0, -second, second)
    return first, second


def fill_table(cols_ref, table_ref, turn_ref, points):
    devices, owned = cols_ref.shape
    factor = math.sqrt(2.0 / points)
    lane = iota((1, 128), 1).astype(F32)
    size = 64

    def body(chunk, carry):
        start = pl.multiple_of(chunk * size, size)
        whole = cols_ref[pl.ds(start, size), :]
        waves = whole.astype(F32)
        half_cos, half_sin = circle(waves, 2 * points)
        sign = 1.0 - 2.0 * (whole & 1).astype(F32)
        gap = jnp.zeros((size, 8 - owned), F32)
        rest = jnp.zeros((size, 128 - 24), F32)
        turn_ref[pl.ds(start, size), :] = jnp.concatenate([half_cos, gap, half_sin, gap, sign, gap, rest], axis=1)
        jump_cos, jump_sin = circle(waves * 256.0, 2 * points)
        for slot in range(owned):
            picked = slice(slot, slot + 1)
            cos0, sin0 = circle(waves[:, picked] * (2.0 * lane + 1.0), 2 * points)
            cos0, sin0 = cos0 * factor, sin0 * factor
            turn_cos = jump_cos[:, picked] + jnp.zeros((1, 128), F32)
            turn_sin = jump_sin[:, picked] + jnp.zeros((1, 128), F32)
            cos1 = cos0 * turn_cos - sin0 * turn_sin
            sin1 = sin0 * turn_cos + cos0 * turn_sin
            twice = 2.0 * turn_cos
            rows = [pl.ds(pl.multiple_of((2 * slot + r) * devices + start, size), size) for r in range(2)]
            for index in range(points // 512):
                window = slice(128 * index, 128 * (index + 1))
                table_ref[rows[0], window] = cos0.astype(BF)
                table_ref[rows[1], window] = sin0.astype(BF)
                cos0, cos1 = cos1, twice * cos1 - cos0
                sin0, sin1 = sin1, twice * sin1 - sin0
        return carry

    lax.fori_loop(0, devices // size, body, 0)


def in_south(owner_ref, turn_ref):
    return (owner_ref[0] >= turn_ref.shape[0] // 2).astype(jnp.int32)


def grid_analysis(field, south, extra, turn_ref, table_ref, rhs_ref, stage_ref, send_ref):
    rows, points = field.shape
    devices = turn_ref.shape[0]
    owned = table_ref.shape[0] // (2 * devices)
    width = points // 4
    rhs_ref[...] = make_rhs(field, south)
    turns = turn_ref[...]
    lanes = iota((1, 128), 1)
    parts = [jnp.zeros((devices, 128), F32) + extra] * SUB
    for slot in range(owned):
        group = slot // 2
        mine = (lanes >= group * rows) & (lanes < (group + 1) * rows)
        sign = turns[:, 16 + slot : 17 + slot]
        sums = []
        for r in range(2):
            first = (2 * slot + r) * devices
            sums.append(project(table_ref[first : first + devices, :], rhs_ref[:, width * r : width * (r + 1)], sign))
        half_cos = turns[:, slot : slot + 1]
        half_sin = turns[:, 8 + slot : 9 + slot]
        turned = [sums[0] * half_cos + sums[1] * half_sin, sums[1] * half_cos - sums[0] * half_sin]
        for r in range(2):
            lines = pltpu.roll(turned[r], group * rows, 1) if group > 0 else turned[r]
            place = 2 * (slot % 2) + r
            parts[place] = jnp.where(mine, lines, parts[place])
    for place in range(SUB):
        stage_ref[pl.ds(place, devices, stride=SUB), :] = parts[place]
    send_ref[...] = stage_ref[...].astype(BF)


def grid_synthesis(received, south, turn_ref, table_ref, stage_ref, rows):
    devices = turn_ref.shape[0]
    owned = table_ref.shape[0] // (2 * devices)
    width = table_ref.shape[1]
    source = iota((128, 128), 0)
    to = iota((128, 128), 1)
    base = jnp.where(to >= 2 * rows, 2 * rows, jnp.where(to >= rows, rows, 0))
    flipped = jnp.where((south > 0) & (to < SPARE), 2 * base + (rows - 1) - to, to)
    picker = jnp.where((source == flipped) & (to < SPARE), 1.0, 0.0).astype(BF)
    stage_ref[...] = mm(received, picker)
    turns = turn_ref[...].T
    totals = [jnp.zeros((2 * rows, width), F32)] * 2
    for part in range(2):
        across = [stage_ref[pl.ds(2 * part + r, devices, stride=SUB), :].T for r in range(2)]
        for group in range(GROUPS):
            slot = 2 * group + part
            if slot < owned:
                cosines, sines = [lines[rows * group : rows * (group + 1)] for lines in across]
                half_cos = turns[slot : slot + 1]
                half_sin = turns[8 + slot : 9 + slot]
                sign = turns[16 + slot : 17 + slot]
                turned = [cosines * half_cos - sines * half_sin, cosines * half_sin + sines * half_cos]
                for r in range(2):
                    lhs = jnp.concatenate([turned[r], turned[r] * sign], axis=0).astype(BF)
                    first = (2 * slot + r) * devices
                    totals[r] = totals[r] + mm(lhs, table_ref[first : first + devices, :])
    ahead = totals[0] + totals[1]
    count = 2 * rows
    back = reverse_lanes(jnp.concatenate(split(totals[0] - totals[1], 3), axis=0).astype(BF))
    back = back[:count] + back[count : 2 * count] + back[2 * count :]
    return jnp.concatenate([ahead[:rows], back[rows:], ahead[rows:], back[:rows]], axis=1)


def first_kernel(owner_ref, cols_ref, inn_hbm, mask_hbm, weight_hbm, basis_hbm,
                 table_ref, turn_ref, basis_ref, scale_ref, send_ref,
                 inn_ref, mask_ref, weight_ref, rhs_ref, stage_ref, sems):
    points = inn_ref.shape[1]
    pairs = ((inn_hbm, inn_ref), (mask_hbm, mask_ref), (weight_hbm, weight_ref), (basis_hbm, basis_ref))
    copies = [pltpu.make_async_copy(a, b, sems.at[i]) for i, (a, b) in enumerate(pairs)]
    for copy in copies:
        copy.start()
    fill_table(cols_ref, table_ref, turn_ref, points)
    for copy in copies[:3]:
        copy.wait()
    scale = mask_ref[...].astype(F32) * weight_ref[...]
    scale_ref[...] = scale
    grid_analysis(scale * inn_ref[...], in_south(owner_ref, turn_ref), jnp.zeros((1, 128), F32),
                  turn_ref, table_ref, rhs_ref, stage_ref, send_ref)
    copies[3].wait()


def middle_kernel(owner_ref, x_ref, table_ref, turn_ref, scale_ref,
                  field_ref, send_ref, scalar_ref, rhs_ref, stage_ref):
    rows = scale_ref.shape[0]
    south = in_south(owner_ref, turn_ref)
    received = x_ref[...]
    (norm0,) = unpack_scalars(received.astype(F32), 1)
    field = grid_synthesis(received, south, turn_ref, table_ref, stage_ref, rows)
    field_ref[...] = field
    scaled = scale_ref[...] * field
    energy = jnp.sum(scaled * field)
    scalar_ref[...] = jnp.zeros((8, 128), F32) + norm0
    grid_analysis(scaled, south, pack_scalars([norm0, energy]), turn_ref, table_ref, rhs_ref, stage_ref, send_ref)


def last_kernel(owner_ref, x_ref, table_ref, turn_ref, scale_ref, first_ref, scalar_in,
                field_ref, energy_ref, scalar_ref, stage_ref):
    rows = scale_ref.shape[0]
    received = x_ref[...]
    norm1, cross = unpack_scalars(received.astype(F32), 2)
    norm0 = scalar_in[0:1, 0:1]
    beta = (jnp.zeros((1, 1), F32) + norm1) / norm0
    field = grid_synthesis(received, in_south(owner_ref, turn_ref), turn_ref, table_ref, stage_ref, rows)
    field = field + beta * first_ref[...]
    field_ref[...] = field
    energy_ref[...] = jnp.zeros(energy_ref.shape, F32) + jnp.sum(scale_ref[...] * field * field)
    line = iota((8, 128), 0)
    scalar_ref[...] = jnp.where(line == 0, norm1, cross)


def lane_windows(band, rows):
    start = band * rows
    block, offset = start // 128, start % 128
    if offset + rows <= 128:
        return [(block, offset, offset + rows)]
    return [(block, offset, 128), (block + 1, 0, offset + rows - 128)]


def parity_row(wave, degrees):
    offset = iota((1, degrees), 1) - wave
    return jnp.where(offset >= 0, 1.0 - 2.0 * (offset & 1).astype(F32), 0.0)


def spectral_kernel(rows, with_base, owner_ref, order_ref, x_ref, basis_ref, spread_ref, *refs):
    if with_base:
        base_ref, across_ref, out_ref, send_ref, scalar_ref, stage_ref = refs
    else:
        out_ref, send_ref, across_ref, stage_ref = refs
    owned, half_rows, degrees = basis_ref.shape
    bands = half_rows // rows
    received = x_ref[...].astype(F32)
    lane = iota((1, 128), 1)
    if with_base:
        norm0, energy = unpack_scalars(received, 2)
        norm0 = (jnp.zeros((1, 1), F32) + norm0) * (1.0 / (2 * bands * 8))
        step_size = norm0 / (norm0 + energy)
        scalar_ref[...] = jnp.zeros((8, 128), F32) + step_size
    spread_rows = jnp.concatenate([spread_ref[...], spread_ref[...]], axis=0)
    stage_ref[...] = received
    senders = [stage_ref[pl.ds(place, 2 * bands * 8, stride=SUB), :] for place in range(SUB)]

    def along(place, group, side):
        columns = [jnp.zeros((8, 128), F32)] * (half_rows // 128)
        for band in range(bands):
            row = band if side == 0 else 2 * bands - 1 - band
            block = senders[place][8 * row : 8 * row + 8]
            shift = (rows * band - rows * group) % 128
            if shift:
                block = pltpu.roll(block, shift, 1)
            for index, low, high in lane_windows(band, rows):
                columns[index] = jnp.where((lane >= low) & (lane < high), block, columns[index])
        return jnp.concatenate(columns, axis=1)

    norm = jnp.zeros((16, degrees), F32)
    cross = jnp.zeros((16, degrees), F32)
    parities = []
    for slot in range(owned):
        parity = parity_row(order_ref[owner_ref[0] * owned + slot], degrees)
        parities.append(parity)
        pieces = [along(2 * (slot % 2) + r, slot // 2, side) for side in range(2) for r in range(2)]
        lhs = jnp.concatenate(pieces, axis=0).astype(BF)
        sums = mm(lhs, basis_ref[slot])
        if not with_base:
            across_ref[slot] = basis_ref[slot].T
        value = (sums[:16] * jnp.abs(parity) + parity * sums[16:]) * spread_rows
        if with_base:
            base = base_ref[slot]
            value = base - step_size * (base + value)
            cross = cross + value * base
        out_ref[slot] = value
        norm = norm + value * value
    if with_base:
        extra = pack_scalars([jnp.sum(norm), jnp.sum(cross)])
    else:
        extra = pack_scalars([jnp.sum(norm)])
    sides = []
    for slot in range(owned):
        parity = parities[slot]
        coeff = (out_ref[slot] * spread_rows * jnp.abs(parity)).astype(BF).astype(F32)
        even = jnp.where(parity > 0, coeff, 0.0)
        odd = jnp.where(parity < 0, coeff, 0.0)
        sums = mm(jnp.concatenate([even, odd], axis=0).astype(BF), across_ref[slot])
        sides.append((sums[:16] + sums[16:], sums[:16] - sums[16:]))
    for side in range(2):
        for band in range(bands):
            row = band if side == 0 else 2 * bands - 1 - band
            for place in range(SUB):
                block = jnp.zeros((8, 128), F32) + extra
                for group in range(GROUPS):
                    slot = 2 * group + place // 2
                    if slot < owned:
                        lines = sides[slot][side][8 * (place % 2) : 8 * (place % 2) + 8]
                        shift = (rows * group - rows * band) % 128
                        start = rows * group
                        for index, low, high in lane_windows(band, rows):
                            source = lines[:, 128 * index : 128 * index + 128]
                            if shift:
                                source = pltpu.roll(source, shift, 1)
                            block = jnp.where((lane >= start) & (lane < start + high - low), source, block)
                            start += high - low
                stage_ref[pl.ds(32 * row + place, 8, stride=SUB), :] = block
    send_ref[...] = stage_ref[...].astype(BF)


def finish_kernel(energy_ref, norm0_ref, norms_ref, step_ref, rhs_ref, residual_ref, field1_ref, field2_ref,
                  control_ref, increment_ref):
    total = jnp.sum(energy_ref[...], axis=0, keepdims=True)[:, 0:1]
    first = norm0_ref[0:1, 0:1]
    norm1 = norms_ref[0:1, 0:1]
    cross = norms_ref[1:2, 0:1]
    step1 = step_ref[0:1, 0:1]
    beta = norm1 / first
    step2 = norm1 / (norm1 + 2.0 * beta * cross + beta * beta * first + total)
    mixed = step1 + step2 * beta
    for slot in range(rhs_ref.shape[0]):
        control_ref[slot] = mixed * rhs_ref[slot] + step2 * residual_ref[slot]
    increment_ref[...] = step1 * field1_ref[...] + step2 * field2_ref[...]


SMEM = pl.BlockSpec(memory_space=pltpu.SMEM)
VMEM = pl.BlockSpec(memory_space=pltpu.VMEM)
HBM = pl.BlockSpec(memory_space=pltpu.HBM)


def near(array):
    return pltpu.with_memory_space_constraint(array, pltpu.VMEM)


def far(array):
    return pltpu.with_memory_space_constraint(array, pltpu.HBM)


def shape(dims, dtype):
    return jax.ShapeDtypeStruct(dims, dtype)


def exchange(buffer):
    return lax.all_to_all(buffer, ("lat", "lev"), split_axis=0, concat_axis=0, tiled=True)


def local(innovation, obs_mask, obs_weight, order, basis, spread):
    lat = lax.axis_index("lat")
    lev = lax.axis_index("lev")
    devices = lax.axis_size("lat") * lax.axis_size("lev")
    owned, half_rows, degrees = basis.shape
    rows, points = innovation.shape[1:]
    chunk_rows = devices * SUB
    owner = (lat * lax.axis_size("lev") + lev).astype(jnp.int32).reshape(1)
    cols = order.reshape(devices, owned)
    table_rows = 2 * owned * devices
    stage = pltpu.VMEM((chunk_rows, 128), F32)
    rhs_part = pltpu.VMEM((256, points // 2), BF)
    plane = (rows, points)

    table, turn, basis, scale, send = pl.pallas_call(
        first_kernel,
        in_specs=[SMEM, VMEM, HBM, HBM, HBM, HBM],
        out_specs=[VMEM] * 5,
        out_shape=[
            pltpu.VMEM((table_rows, points // 4), BF),
            pltpu.VMEM((devices, 128), F32),
            pltpu.VMEM(basis.shape, BF),
            pltpu.VMEM(plane, F32),
            shape((chunk_rows, 128), BF),
        ],
        scratch_shapes=[pltpu.VMEM(plane, F32), pltpu.VMEM(plane, jnp.int32), pltpu.VMEM(plane, F32)]
        + [rhs_part, stage, pltpu.SemaphoreType.DMA((4,))],
        compiler_params=params(),
        name="first",
    )(owner, cols, *map(far, (innovation.reshape(plane), obs_mask.reshape(plane), obs_weight.reshape(plane), basis)))
    table, turn, basis, scale = map(near, (table, turn, basis, scale))

    def spectral(received, *more):
        with_base = len(more) > 0
        return pl.pallas_call(
            functools.partial(spectral_kernel, rows, with_base),
            in_specs=[SMEM, SMEM, VMEM, VMEM, VMEM] + [VMEM] * len(more),
            out_specs=[VMEM] * 3,
            out_shape=[shape((owned, 16, degrees), F32), shape((chunk_rows, 128), BF)]
            + [shape((8, 128), F32) if with_base else pltpu.VMEM((owned, degrees, half_rows), BF)],
            scratch_shapes=[stage],
            compiler_params=params(),
            name="spectral",
        )(owner, order, received, basis, spread, *more)

    rhs, send, across = spectral(exchange(send))
    across = near(across)
    field1, send, norm0 = pl.pallas_call(
        middle_kernel,
        in_specs=[SMEM, VMEM, VMEM, VMEM, VMEM],
        out_specs=[VMEM] * 3,
        out_shape=[shape(plane, F32), shape((chunk_rows, 128), BF), shape((8, 128), F32)],
        scratch_shapes=[rhs_part, stage],
        compiler_params=params(),
        name="middle",
    )(owner, exchange(send), table, turn, scale)
    residual, send, step1 = spectral(exchange(send), rhs, across)
    field2, energy, norms = pl.pallas_call(
        last_kernel,
        in_specs=[SMEM] + [VMEM] * 6,
        out_specs=[VMEM] * 3,
        out_shape=[shape(plane, F32), shape((devices, 128), F32), shape((8, 128), F32)],
        scratch_shapes=[stage],
        compiler_params=params(),
        name="last",
    )(owner, exchange(send), table, turn, scale, field1, norm0)
    control, increment = pl.pallas_call(
        finish_kernel,
        in_specs=[VMEM] * 8,
        out_specs=[VMEM] * 2,
        out_shape=[shape(rhs.shape, F32), shape(plane, F32)],
        compiler_params=params(),
        name="finish",
    )(exchange(energy), norm0, norms, step1, rhs, residual, field1, field2)
    return (control, increment.reshape(innovation.shape))


def solution(mesh):
    in_specs = (
        P("lev", "lat", None),
        P("lev", "lat", None),
        P("lev", "lat", None),
        P(),
        P(("lat", "lev"), None, None),
        P(),
    )
    out_specs = (P(("lat", "lev"), None, None), P("lev", "lat", None))
    return jax.shard_map(local, mesh=mesh, in_specs=in_specs, out_specs=out_specs, check_vma=False)
```

```python
import functools
import math

import jax
import jax.numpy as jnp
from jax import lax
from jax.experimental import pallas as pl
from jax.experimental.pallas import tpu as pltpu
from jax.sharding import PartitionSpec as P

BF = jnp.bfloat16
F32 = jnp.float32
GROUPS = 3
SUB = 4
SPARE = 120
VMEM_LIMIT = 20 * 1024 * 1024


def iota(shape, axis):
    return lax.broadcasted_iota(jnp.int32, shape, axis)


def params():
    return pltpu.CompilerParams(vmem_limit_bytes=VMEM_LIMIT)


def mm(a, b):
    return jnp.dot(a, b, preferred_element_type=F32)


def mm_nt(a, b):
    return lax.dot_general(a, b, (((1,), (1,)), ((), ())), preferred_element_type=F32)


def pack_scalars(values):
    lane = iota((1, 128), 1)
    out = jnp.zeros((1, 128), F32)
    for index, value in enumerate(values):
        rest = jnp.zeros((1, 128), F32) + value
        for piece in range(3):
            part = rest.astype(BF).astype(F32)
            rest = rest - part
            out = jnp.where(lane == SPARE + 3 * index + piece, part, out)
    return out


def unpack_scalars(received, count):
    total = jnp.sum(received, axis=0, keepdims=True) * (1.0 / SUB)
    lane = iota((1, 128), 1)
    sums = []
    for index in range(count):
        first = SPARE + 3 * index
        sums.append(jnp.sum(jnp.where((lane >= first) & (lane < first + 3), total, 0.0)))
    return sums


def reverse_lanes(pieces):
    width = pieces.shape[1]
    flip = jnp.where(iota((128, 128), 0) + iota((128, 128), 1) == 127, 1.0, 0.0).astype(BF)
    return jnp.concatenate([mm(pieces[:, first : first + 128], flip) for first in range(width - 128, -1, -128)], axis=1)


def split(values, count):
    pieces = []
    for _ in range(count):
        pieces.append(values.astype(BF).astype(F32))
        values = values - pieces[-1]
    return pieces


def make_rhs(field, south):
    rows, points = field.shape
    width = points // 4
    quarters = [field[:, width * i : width * (i + 1)] for i in range(4)]
    pieces = split(quarters[1], 2) + split(quarters[3], 2)
    back = reverse_lanes(jnp.concatenate(pieces, axis=0).astype(BF))
    back1 = back[:rows] + back[rows : 2 * rows]
    back3 = back[2 * rows : 3 * rows] + back[3 * rows :]
    gap = jnp.zeros((64 - rows, width), F32)

    def bands(plain, signed):
        parts = []
        for piece in split(plain, 2) + split(signed, 2):
            parts += [piece, gap]
        return jnp.concatenate(parts, axis=0)

    stacked = jnp.concatenate(
        [bands(quarters[0] + back3, quarters[2] + back1), bands(quarters[0] - back3, quarters[2] - back1)], axis=1
    ).astype(BF)
    to = iota((256, 256), 0)
    source = iota((256, 256), 1)
    inner = to & 63
    flipped = jnp.where((south > 0) & (inner < rows), to - inner + (rows - 1) - inner, to)
    picker = jnp.where(source == flipped, 1.0, 0.0).astype(BF)
    return mm(picker, stacked).astype(BF)


def project(table, rhs, sign):
    product = mm_nt(table, rhs)
    both = product[:, :128] + sign * product[:, 128:]
    return both + pltpu.roll(both, 64, 1)


def circle(steps, points):
    turns = jnp.floor(steps * (1.0 / points) + 0.5)
    angle = (steps - turns * points) * (0.5 * math.pi / points)
    square = angle * angle
    sine = jnp.full_like(square, 1.0 / 362880.0)
    for coefficient in (-1.0 / 5040.0, 1.0 / 120.0, -1.0 / 6.0, 1.0):
        sine = sine * square + coefficient
    sine = sine * angle
    cosine = jnp.full_like(square, 1.0 / 40320.0)
    for coefficient in (-1.0 / 720.0, 1.0 / 24.0, -0.5, 1.0):
        cosine = cosine * square + coefficient
    for _ in range(2):
        twice = sine + sine
        cosine, sine = 1.0 - twice * sine, twice * cosine
    return cosine, sine


def fill_table(cols_ref, table_ref, turn_ref, points):
    devices, owned = cols_ref.shape
    factor = math.sqrt(2.0 / points)
    lane = iota((1, 128), 1).astype(F32)
    size = 64

    def body(chunk, carry):
        start = pl.multiple_of(chunk * size, size)
        whole = cols_ref[pl.ds(start, size), :]
        waves = whole.astype(F32)
        half_cos, half_sin = circle(waves, 2 * points)
        sign = 1.0 - 2.0 * (whole & 1).astype(F32)
        gap = jnp.zeros((size, 8 - owned), F32)
        rest = jnp.zeros((size, 128 - 24), F32)
        turn_ref[pl.ds(start, size), :] = jnp.concatenate([half_cos, gap, half_sin, gap, sign, gap, rest], axis=1)
        jump_cos, jump_sin = circle(waves * 256.0, 2 * points)
        for slot in range(owned):
            picked = slice(slot, slot + 1)
            cos0, sin0 = circle(waves[:, picked] * (2.0 * lane + 1.0), 2 * points)
            cos0, sin0 = cos0 * factor, sin0 * factor
            turn_cos = jump_cos[:, picked] + jnp.zeros((1, 128), F32)
            turn_sin = jump_sin[:, picked] + jnp.zeros((1, 128), F32)
            cos1 = cos0 * turn_cos - sin0 * turn_sin
            sin1 = sin0 * turn_cos + cos0 * turn_sin
            twice = 2.0 * turn_cos
            rows = [pl.ds(pl.multiple_of((2 * slot + r) * devices + start, size), size) for r in range(2)]
            for index in range(points // 512):
                window = slice(128 * index, 128 * (index + 1))
                table_ref[rows[0], window] = cos0.astype(BF)
                table_ref[rows[1], window] = sin0.astype(BF)
                cos0, cos1 = cos1, twice * cos1 - cos0
                sin0, sin1 = sin1, twice * sin1 - sin0
        return carry

    lax.fori_loop(0, devices // size, body, 0)


def in_south(owner_ref, turn_ref):
    return (owner_ref[0] >= turn_ref.shape[0] // 2).astype(jnp.int32)


def grid_analysis(field, south, extra, turn_ref, table_ref, rhs_ref, stage_ref, send_ref):
    rows, points = field.shape
    devices = turn_ref.shape[0]
    owned = table_ref.shape[0] // (2 * devices)
    width = points // 4
    rhs_ref[...] = make_rhs(field, south)
    turns = turn_ref[...]
    lanes = iota((1, 128), 1)
    parts = [jnp.zeros((devices, 128), F32) + extra] * SUB
    for slot in range(owned):
        group = slot // 2
        mine = (lanes >= group * rows) & (lanes < (group + 1) * rows)
        sign = turns[:, 16 + slot : 17 + slot]
        sums = []
        for r in range(2):
            first = (2 * slot + r) * devices
            sums.append(project(table_ref[first : first + devices, :], rhs_ref[:, width * r : width * (r + 1)], sign))
        half_cos = turns[:, slot : slot + 1]
        half_sin = turns[:, 8 + slot : 9 + slot]
        turned = [sums[0] * half_cos + sums[1] * half_sin, sums[1] * half_cos - sums[0] * half_sin]
        for r in range(2):
            lines = pltpu.roll(turned[r], group * rows, 1) if group > 0 else turned[r]
            place = 2 * (slot % 2) + r
            parts[place] = jnp.where(mine, lines, parts[place])
    for place in range(SUB):
        stage_ref[pl.ds(place, devices, stride=SUB), :] = parts[place]
    send_ref[...] = stage_ref[...].astype(BF)


def grid_synthesis(received, south, turn_ref, table_ref, stage_ref, rows):
    devices = turn_ref.shape[0]
    owned = table_ref.shape[0] // (2 * devices)
    width = table_ref.shape[1]
    source = iota((128, 128), 0)
    to = iota((128, 128), 1)
    base = jnp.where(to >= 2 * rows, 2 * rows, jnp.where(to >= rows, rows, 0))
    flipped = jnp.where((south > 0) & (to < SPARE), 2 * base + (rows - 1) - to, to)
    picker = jnp.where((source == flipped) & (to < SPARE), 1.0, 0.0).astype(BF)
    stage_ref[...] = mm(received, picker)
    turns = turn_ref[...].T
    totals = [jnp.zeros((2 * rows, width), F32)] * 2
    for part in range(2):
        across = [stage_ref[pl.ds(2 * part + r, devices, stride=SUB), :].T for r in range(2)]
        for group in range(GROUPS):
            slot = 2 * group + part
            if slot < owned:
                cosines, sines = [lines[rows * group : rows * (group + 1)] for lines in across]
                half_cos = turns[slot : slot + 1]
                half_sin = turns[8 + slot : 9 + slot]
                sign = turns[16 + slot : 17 + slot]
                turned = [cosines * half_cos - sines * half_sin, cosines * half_sin + sines * half_cos]
                for r in range(2):
                    lhs = jnp.concatenate([turned[r], turned[r] * sign], axis=0).astype(BF)
                    first = (2 * slot + r) * devices
                    totals[r] = totals[r] + mm(lhs, table_ref[first : first + devices, :])
    ahead = totals[0] + totals[1]
    count = 2 * rows
    back = reverse_lanes(jnp.concatenate(split(totals[0] - totals[1], 3), axis=0).astype(BF))
    back = back[:count] + back[count : 2 * count] + back[2 * count :]
    return jnp.concatenate([ahead[:rows], back[rows:], ahead[rows:], back[:rows]], axis=1)


def first_kernel(owner_ref, cols_ref, inn_hbm, mask_hbm, weight_hbm, basis_hbm,
                 table_ref, turn_ref, basis_ref, scale_ref, send_ref,
                 inn_ref, mask_ref, weight_ref, rhs_ref, stage_ref, sems):
    points = inn_ref.shape[1]
    pairs = ((inn_hbm, inn_ref), (mask_hbm, mask_ref), (weight_hbm, weight_ref), (basis_hbm, basis_ref))
    copies = [pltpu.make_async_copy(a, b, sems.at[i]) for i, (a, b) in enumerate(pairs)]
    for copy in copies:
        copy.start()
    fill_table(cols_ref, table_ref, turn_ref, points)
    for copy in copies[:3]:
        copy.wait()
    scale = mask_ref[...].astype(F32) * weight_ref[...]
    scale_ref[...] = scale
    grid_analysis(scale * inn_ref[...], in_south(owner_ref, turn_ref), jnp.zeros((1, 128), F32),
                  turn_ref, table_ref, rhs_ref, stage_ref, send_ref)
    copies[3].wait()


def middle_kernel(owner_ref, x_ref, table_ref, turn_ref, scale_ref,
                  field_ref, send_ref, scalar_ref, rhs_ref, stage_ref):
    rows = scale_ref.shape[0]
    south = in_south(owner_ref, turn_ref)
    received = x_ref[...]
    (norm0,) = unpack_scalars(received.astype(F32), 1)
    field = grid_synthesis(received, south, turn_ref, table_ref, stage_ref, rows)
    field_ref[...] = field
    scaled = scale_ref[...] * field
    energy = jnp.sum(scaled * field)
    scalar_ref[...] = jnp.zeros((8, 128), F32) + norm0
    grid_analysis(scaled, south, pack_scalars([norm0, energy]), turn_ref, table_ref, rhs_ref, stage_ref, send_ref)


def last_kernel(owner_ref, x_ref, table_ref, turn_ref, scale_ref, first_ref, scalar_in,
                field_ref, energy_ref, scalar_ref, stage_ref):
    rows = scale_ref.shape[0]
    received = x_ref[...]
    norm1, cross = unpack_scalars(received.astype(F32), 2)
    norm0 = scalar_in[0:1, 0:1]
    beta = (jnp.zeros((1, 1), F32) + norm1) / norm0
    field = grid_synthesis(received, in_south(owner_ref, turn_ref), turn_ref, table_ref, stage_ref, rows)
    field = field + beta * first_ref[...]
    field_ref[...] = field
    energy_ref[...] = jnp.zeros(energy_ref.shape, F32) + jnp.sum(scale_ref[...] * field * field)
    line = iota((8, 128), 0)
    scalar_ref[...] = jnp.where(line == 0, norm1, cross)


def lane_windows(band, rows):
    start = band * rows
    block, offset = start // 128, start % 128
    if offset + rows <= 128:
        return [(block, offset, offset + rows)]
    return [(block, offset, 128), (block + 1, 0, offset + rows - 128)]


def parity_row(wave, degrees):
    offset = iota((1, degrees), 1) - wave
    return jnp.where(offset >= 0, 1.0 - 2.0 * (offset & 1).astype(F32), 0.0)


def spectral_kernel(rows, with_base, owner_ref, order_ref, x_ref, basis_ref, spread_ref, *refs):
    if with_base:
        base_ref, across_ref, out_ref, send_ref, scalar_ref, stage_ref = refs
    else:
        out_ref, send_ref, across_ref, stage_ref = refs
    owned, half_rows, degrees = basis_ref.shape
    bands = half_rows // rows
    received = x_ref[...].astype(F32)
    lane = iota((1, 128), 1)
    if with_base:
        norm0, energy = unpack_scalars(received, 2)
        norm0 = (jnp.zeros((1, 1), F32) + norm0) * (1.0 / (2 * bands * 8))
        step_size = norm0 / (norm0 + energy)
        scalar_ref[...] = jnp.zeros((8, 128), F32) + step_size
    spread_rows = jnp.concatenate([spread_ref[...], spread_ref[...]], axis=0)
    stage_ref[...] = received
    senders = [stage_ref[pl.ds(place, 2 * bands * 8, stride=SUB), :] for place in range(SUB)]

    def along(place, group, side):
        columns = [jnp.zeros((8, 128), F32)] * (half_rows // 128)
        for band in range(bands):
            row = band if side == 0 else 2 * bands - 1 - band
            block = senders[place][8 * row : 8 * row + 8]
            shift = (rows * band - rows * group) % 128
            if shift:
                block = pltpu.roll(block, shift, 1)
            for index, low, high in lane_windows(band, rows):
                columns[index] = jnp.where((lane >= low) & (lane < high), block, columns[index])
        return jnp.concatenate(columns, axis=1)

    norm = jnp.zeros((16, degrees), F32)
    cross = jnp.zeros((16, degrees), F32)
    parities = []
    for slot in range(owned):
        parity = parity_row(order_ref[owner_ref[0] * owned + slot], degrees)
        parities.append(parity)
        pieces = [along(2 * (slot % 2) + r, slot // 2, side) for side in range(2) for r in range(2)]
        lhs = jnp.concatenate(pieces, axis=0).astype(BF)
        sums = mm(lhs, basis_ref[slot])
        if not with_base:
            across_ref[slot] = basis_ref[slot].T
        value = (sums[:16] * jnp.abs(parity) + parity * sums[16:]) * spread_rows
        if with_base:
            base = base_ref[slot]
            value = base - step_size * (base + value)
            cross = cross + value * base
        out_ref[slot] = value
        norm = norm + value * value
    if with_base:
        extra = pack_scalars([jnp.sum(norm), jnp.sum(cross)])
    else:
        extra = pack_scalars([jnp.sum(norm)])
    for slot in range(owned):
        parity = parities[slot]
        coeff = (out_ref[slot] * spread_rows * jnp.abs(parity)).astype(BF).astype(F32)
        even = jnp.where(parity > 0, coeff, 0.0)
        odd = jnp.where(parity < 0, coeff, 0.0)
        sums = mm(jnp.concatenate([even, odd], axis=0).astype(BF), across_ref[slot])
        sides = (sums[:16] + sums[16:], sums[:16] - sums[16:])
        group = slot // 2
        for side in range(2):
            for band in range(bands):
                row = band if side == 0 else 2 * bands - 1 - band
                for r in range(2):
                    lines = sides[side][8 * r : 8 * r + 8]
                    window = pl.ds(32 * row + 2 * (slot % 2) + r, 8, stride=SUB)
                    block = stage_ref[window, :] if group > 0 else jnp.zeros((8, 128), F32) + extra
                    shift = (rows * group - rows * band) % 128
                    start = rows * group
                    for index, low, high in lane_windows(band, rows):
                        source = lines[:, 128 * index : 128 * index + 128]
                        if shift:
                            source = pltpu.roll(source, shift, 1)
                        block = jnp.where((lane >= start) & (lane < start + high - low), source, block)
                        start += high - low
                    stage_ref[window, :] = block
    send_ref[...] = stage_ref[...].astype(BF)


def finish_kernel(energy_ref, norm0_ref, norms_ref, step_ref, rhs_ref, residual_ref, field1_ref, field2_ref,
                  control_ref, increment_ref):
    total = jnp.sum(energy_ref[...], axis=0, keepdims=True)[:, 0:1]
    first = norm0_ref[0:1, 0:1]
    norm1 = norms_ref[0:1, 0:1]
    cross = norms_ref[1:2, 0:1]
    step1 = step_ref[0:1, 0:1]
    beta = norm1 / first
    step2 = norm1 / (norm1 + 2.0 * beta * cross + beta * beta * first + total)
    mixed = step1 + step2 * beta
    for slot in range(rhs_ref.shape[0]):
        control_ref[slot] = mixed * rhs_ref[slot] + step2 * residual_ref[slot]
    increment_ref[...] = step1 * field1_ref[...] + step2 * field2_ref[...]


SMEM = pl.BlockSpec(memory_space=pltpu.SMEM)
VMEM = pl.BlockSpec(memory_space=pltpu.VMEM)
HBM = pl.BlockSpec(memory_space=pltpu.HBM)


def near(array):
    return pltpu.with_memory_space_constraint(array, pltpu.VMEM)


def far(array):
    return pltpu.with_memory_space_constraint(array, pltpu.HBM)


def shape(dims, dtype):
    return jax.ShapeDtypeStruct(dims, dtype)


def exchange(buffer):
    return lax.all_to_all(buffer, ("lat", "lev"), split_axis=0, concat_axis=0, tiled=True)


def local(innovation, obs_mask, obs_weight, order, basis, spread):
    lat = lax.axis_index("lat")
    lev = lax.axis_index("lev")
    devices = lax.axis_size("lat") * lax.axis_size("lev")
    owned, half_rows, degrees = basis.shape
    rows, points = innovation.shape[1:]
    chunk_rows = devices * SUB
    owner = (lat * lax.axis_size("lev") + lev).astype(jnp.int32).reshape(1)
    cols = order.reshape(devices, owned)
    table_rows = 2 * owned * devices
    stage = pltpu.VMEM((chunk_rows, 128), F32)
    rhs_part = pltpu.VMEM((256, points // 2), BF)
    plane = (rows, points)

    table, turn, basis, scale, send = pl.pallas_call(
        first_kernel,
        in_specs=[SMEM, VMEM, HBM, HBM, HBM, HBM],
        out_specs=[VMEM] * 5,
        out_shape=[
            pltpu.VMEM((table_rows, points // 4), BF),
            pltpu.VMEM((devices, 128), F32),
            pltpu.VMEM(basis.shape, BF),
            pltpu.VMEM(plane, F32),
            shape((chunk_rows, 128), BF),
        ],
        scratch_shapes=[pltpu.VMEM(plane, F32), pltpu.VMEM(plane, jnp.int32), pltpu.VMEM(plane, F32)]
        + [rhs_part, stage, pltpu.SemaphoreType.DMA((4,))],
        compiler_params=params(),
        name="first",
    )(owner, cols, *map(far, (innovation.reshape(plane), obs_mask.reshape(plane), obs_weight.reshape(plane), basis)))
    table, turn, basis, scale = map(near, (table, turn, basis, scale))

    def spectral(received, *more):
        with_base = len(more) > 0
        return pl.pallas_call(
            functools.partial(spectral_kernel, rows, with_base),
            in_specs=[SMEM, SMEM, VMEM, VMEM, VMEM] + [VMEM] * len(more),
            out_specs=[VMEM] * 3,
            out_shape=[shape((owned, 16, degrees), F32), shape((chunk_rows, 128), BF)]
            + [shape((8, 128), F32) if with_base else pltpu.VMEM((owned, degrees, half_rows), BF)],
            scratch_shapes=[stage],
            compiler_params=params(),
            name="spectral",
        )(owner, order, received, basis, spread, *more)

    rhs, send, across = spectral(exchange(send))
    across = near(across)
    field1, send, norm0 = pl.pallas_call(
        middle_kernel,
        in_specs=[SMEM, VMEM, VMEM, VMEM, VMEM],
        out_specs=[VMEM] * 3,
        out_shape=[shape(plane, F32), shape((chunk_rows, 128), BF), shape((8, 128), F32)],
        scratch_shapes=[rhs_part, stage],
        compiler_params=params(),
        name="middle",
    )(owner, exchange(send), table, turn, scale)
    residual, send, step1 = spectral(exchange(send), rhs, across)
    field2, energy, norms = pl.pallas_call(
        last_kernel,
        in_specs=[SMEM] + [VMEM] * 6,
        out_specs=[VMEM] * 3,
        out_shape=[shape(plane, F32), shape((devices, 128), F32), shape((8, 128), F32)],
        scratch_shapes=[stage],
        compiler_params=params(),
        name="last",
    )(owner, exchange(send), table, turn, scale, field1, norm0)
    control, increment = pl.pallas_call(
        finish_kernel,
        in_specs=[VMEM] * 8,
        out_specs=[VMEM] * 2,
        out_shape=[shape(rhs.shape, F32), shape(plane, F32)],
        compiler_params=params(),
        name="finish",
    )(exchange(energy), norm0, norms, step1, rhs, residual, field1, field2)
    return (control, increment.reshape(innovation.shape))


def solution(mesh):
    in_specs = (
        P("lev", "lat", None),
        P("lev", "lat", None),
        P("lev", "lat", None),
        P(),
        P(("lat", "lev"), None, None),
        P(),
    )
    out_specs = (P(("lat", "lev"), None, None), P("lev", "lat", None))
    return jax.shard_map(local, mesh=mesh, in_specs=in_specs, out_specs=out_specs, check_vma=False)
```

```python
import functools
import math

import jax
import jax.numpy as jnp
from jax import lax
from jax.experimental import pallas as pl
from jax.experimental.pallas import tpu as pltpu
from jax.sharding import PartitionSpec as P

BF = jnp.bfloat16
F32 = jnp.float32
GROUPS = 3
SUB = 4
SPARE = 120
VMEM_LIMIT = 20 * 1024 * 1024


def iota(shape, axis):
    return lax.broadcasted_iota(jnp.int32, shape, axis)


def params():
    return pltpu.CompilerParams(vmem_limit_bytes=VMEM_LIMIT)


def mm(a, b):
    return jnp.dot(a, b, preferred_element_type=F32)


def mm_nt(a, b):
    return lax.dot_general(a, b, (((1,), (1,)), ((), ())), preferred_element_type=F32)


def pack_scalars(values):
    lane = iota((1, 128), 1)
    out = jnp.zeros((1, 128), F32)
    for index, value in enumerate(values):
        rest = jnp.zeros((1, 128), F32) + value
        for piece in range(3):
            part = rest.astype(BF).astype(F32)
            rest = rest - part
            out = jnp.where(lane == SPARE + 3 * index + piece, part, out)
    return out


def unpack_scalars(received, count):
    total = jnp.sum(received, axis=0, keepdims=True) * (1.0 / SUB)
    lane = iota((1, 128), 1)
    sums = []
    for index in range(count):
        first = SPARE + 3 * index
        sums.append(jnp.sum(jnp.where((lane >= first) & (lane < first + 3), total, 0.0)))
    return sums


def reverse_lanes(pieces):
    width = pieces.shape[1]
    flip = jnp.where(iota((128, 128), 0) + iota((128, 128), 1) == 127, 1.0, 0.0).astype(BF)
    return jnp.concatenate([mm(pieces[:, first : first + 128], flip) for first in range(width - 128, -1, -128)], axis=1)


def split(values, count):
    pieces = []
    for _ in range(count):
        pieces.append(values.astype(BF).astype(F32))
        values = values - pieces[-1]
    return pieces


def make_rhs(field, south):
    rows, points = field.shape
    width = points // 4
    quarters = [field[:, width * i : width * (i + 1)] for i in range(4)]
    pieces = split(quarters[1], 2) + split(quarters[3], 2)
    back = reverse_lanes(jnp.concatenate(pieces, axis=0).astype(BF))
    back1 = back[:rows] + back[rows : 2 * rows]
    back3 = back[2 * rows : 3 * rows] + back[3 * rows :]
    gap = jnp.zeros((64 - rows, width), F32)

    def bands(plain, signed):
        parts = []
        for piece in split(plain, 2) + split(signed, 2):
            parts += [piece, gap]
        return jnp.concatenate(parts, axis=0)

    stacked = jnp.concatenate(
        [bands(quarters[0] + back3, quarters[2] + back1), bands(quarters[0] - back3, quarters[2] - back1)], axis=1
    ).astype(BF)
    to = iota((256, 256), 0)
    source = iota((256, 256), 1)
    inner = to & 63
    flipped = jnp.where((south > 0) & (inner < rows), to - inner + (rows - 1) - inner, to)
    picker = jnp.where(source == flipped, 1.0, 0.0).astype(BF)
    return mm(picker, stacked).astype(BF)


def project(table, rhs, sign):
    product = mm_nt(table, rhs)
    both = product[:, :128] + sign * product[:, 128:]
    return both + pltpu.roll(both, 64, 1)


def circle(steps, points):
    turns = jnp.floor(steps * (1.0 / points) + 0.5)
    angle = (steps - turns * points) * (0.5 * math.pi / points)
    square = angle * angle
    sine = jnp.full_like(square, 1.0 / 362880.0)
    for coefficient in (-1.0 / 5040.0, 1.0 / 120.0, -1.0 / 6.0, 1.0):
        sine = sine * square + coefficient
    sine = sine * angle
    cosine = jnp.full_like(square, 1.0 / 40320.0)
    for coefficient in (-1.0 / 720.0, 1.0 / 24.0, -0.5, 1.0):
        cosine = cosine * square + coefficient
    for _ in range(2):
        twice = sine + sine
        cosine, sine = 1.0 - twice * sine, twice * cosine
    return cosine, sine


def fill_table(cols_ref, table_ref, turn_ref, points):
    devices, owned = cols_ref.shape
    factor = math.sqrt(2.0 / points)
    lane = iota((1, 128), 1).astype(F32)
    size = 32

    def body(chunk, carry):
        start = pl.multiple_of(chunk * size, size)
        whole = cols_ref[pl.ds(start, size), :]
        waves = whole.astype(F32)
        half_cos, half_sin = circle(waves, 2 * points)
        sign = 1.0 - 2.0 * (whole & 1).astype(F32)
        gap = jnp.zeros((size, 8 - owned), F32)
        rest = jnp.zeros((size, 128 - 24), F32)
        turn_ref[pl.ds(start, size), :] = jnp.concatenate([half_cos, gap, half_sin, gap, sign, gap, rest], axis=1)
        jump_cos, jump_sin = circle(waves * 256.0, 2 * points)
        for slot in range(owned):
            picked = slice(slot, slot + 1)
            cos0, sin0 = circle(waves[:, picked] * (2.0 * lane + 1.0), 2 * points)
            cos0, sin0 = cos0 * factor, sin0 * factor
            turn_cos = jump_cos[:, picked] + jnp.zeros((1, 128), F32)
            turn_sin = jump_sin[:, picked] + jnp.zeros((1, 128), F32)
            cos1 = cos0 * turn_cos - sin0 * turn_sin
            sin1 = sin0 * turn_cos + cos0 * turn_sin
            twice = 2.0 * turn_cos
            rows = [pl.ds(pl.multiple_of((2 * slot + r) * devices + start, size), size) for r in range(2)]
            for index in range(points // 512):
                window = slice(128 * index, 128 * (index + 1))
                table_ref[rows[0], window] = cos0.astype(BF)
                table_ref[rows[1], window] = sin0.astype(BF)
                cos0, cos1 = cos1, twice * cos1 - cos0
                sin0, sin1 = sin1, twice * sin1 - sin0
        return carry

    lax.fori_loop(0, devices // size, body, 0)


def in_south(owner_ref, turn_ref):
    return (owner_ref[0] >= turn_ref.shape[0] // 2).astype(jnp.int32)


def grid_analysis(field, south, extra, turn_ref, table_ref, rhs_ref, stage_ref, send_ref):
    rows, points = field.shape
    devices = turn_ref.shape[0]
    owned = table_ref.shape[0] // (2 * devices)
    width = points // 4
    rhs_ref[...] = make_rhs(field, south)
    turns = turn_ref[...]
    lanes = iota((1, 128), 1)
    parts = [jnp.zeros((devices, 128), F32) + extra] * SUB
    for slot in range(owned):
        group = slot // 2
        mine = (lanes >= group * rows) & (lanes < (group + 1) * rows)
        sign = turns[:, 16 + slot : 17 + slot]
        sums = []
        for r in range(2):
            first = (2 * slot + r) * devices
            sums.append(project(table_ref[first : first + devices, :], rhs_ref[:, width * r : width * (r + 1)], sign))
        half_cos = turns[:, slot : slot + 1]
        half_sin = turns[:, 8 + slot : 9 + slot]
        turned = [sums[0] * half_cos + sums[1] * half_sin, sums[1] * half_cos - sums[0] * half_sin]
        for r in range(2):
            lines = pltpu.roll(turned[r], group * rows, 1) if group > 0 else turned[r]
            place = 2 * (slot % 2) + r
            parts[place] = jnp.where(mine, lines, parts[place])
    for place in range(SUB):
        stage_ref[pl.ds(place, devices, stride=SUB), :] = parts[place]
    send_ref[...] = stage_ref[...].astype(BF)


def grid_synthesis(received, south, turn_ref, table_ref, stage_ref, rows):
    devices = turn_ref.shape[0]
    owned = table_ref.shape[0] // (2 * devices)
    width = table_ref.shape[1]
    source = iota((128, 128), 0)
    to = iota((128, 128), 1)
    base = jnp.where(to >= 2 * rows, 2 * rows, jnp.where(to >= rows, rows, 0))
    flipped = jnp.where((south > 0) & (to < SPARE), 2 * base + (rows - 1) - to, to)
    picker = jnp.where((source == flipped) & (to < SPARE), 1.0, 0.0).astype(BF)
    stage_ref[...] = mm(received, picker)
    turns = turn_ref[...].T
    totals = [jnp.zeros((2 * rows, width), F32)] * 2
    for part in range(2):
        across = [stage_ref[pl.ds(2 * part + r, devices, stride=SUB), :].T for r in range(2)]
        for group in range(GROUPS):
            slot = 2 * group + part
            if slot < owned:
                cosines, sines = [lines[rows * group : rows * (group + 1)] for lines in across]
                half_cos = turns[slot : slot + 1]
                half_sin = turns[8 + slot : 9 + slot]
                sign = turns[16 + slot : 17 + slot]
                turned = [cosines * half_cos - sines * half_sin, cosines * half_sin + sines * half_cos]
                for r in range(2):
                    lhs = jnp.concatenate([turned[r], turned[r] * sign], axis=0).astype(BF)
                    first = (2 * slot + r) * devices
                    totals[r] = totals[r] + mm(lhs, table_ref[first : first + devices, :])
    ahead = totals[0] + totals[1]
    count = 2 * rows
    back = reverse_lanes(jnp.concatenate(split(totals[0] - totals[1], 3), axis=0).astype(BF))
    back = back[:count] + back[count : 2 * count] + back[2 * count :]
    return jnp.concatenate([ahead[:rows], back[rows:], ahead[rows:], back[:rows]], axis=1)


def first_kernel(owner_ref, cols_ref, inn_hbm, mask_hbm, weight_hbm, basis_hbm,
                 table_ref, turn_ref, basis_ref, scale_ref, send_ref,
                 inn_ref, mask_ref, weight_ref, rhs_ref, stage_ref, sems):
    points = inn_ref.shape[1]
    pairs = ((inn_hbm, inn_ref), (mask_hbm, mask_ref), (weight_hbm, weight_ref), (basis_hbm, basis_ref))
    copies = [pltpu.make_async_copy(a, b, sems.at[i]) for i, (a, b) in enumerate(pairs)]
    for copy in copies:
        copy.start()
    fill_table(cols_ref, table_ref, turn_ref, points)
    for copy in copies[:3]:
        copy.wait()
    scale = mask_ref[...].astype(F32) * weight_ref[...]
    scale_ref[...] = scale
    grid_analysis(scale * inn_ref[...], in_south(owner_ref, turn_ref), jnp.zeros((1, 128), F32),
                  turn_ref, table_ref, rhs_ref, stage_ref, send_ref)
    copies[3].wait()


def middle_kernel(owner_ref, x_ref, table_ref, turn_ref, scale_ref,
                  field_ref, send_ref, scalar_ref, rhs_ref, stage_ref):
    rows = scale_ref.shape[0]
    south = in_south(owner_ref, turn_ref)
    received = x_ref[...]
    (norm0,) = unpack_scalars(received.astype(F32), 1)
    field = grid_synthesis(received, south, turn_ref, table_ref, stage_ref, rows)
    field_ref[...] = field
    scaled = scale_ref[...] * field
    energy = jnp.sum(scaled * field)
    scalar_ref[...] = jnp.zeros((8, 128), F32) + norm0
    grid_analysis(scaled, south, pack_scalars([norm0, energy]), turn_ref, table_ref, rhs_ref, stage_ref, send_ref)


def last_kernel(owner_ref, x_ref, table_ref, turn_ref, scale_ref, first_ref, scalar_in,
                field_ref, energy_ref, scalar_ref, stage_ref):
    rows = scale_ref.shape[0]
    received = x_ref[...]
    norm1, cross = unpack_scalars(received.astype(F32), 2)
    norm0 = scalar_in[0:1, 0:1]
    beta = (jnp.zeros((1, 1), F32) + norm1) / norm0
    field = grid_synthesis(received, in_south(owner_ref, turn_ref), turn_ref, table_ref, stage_ref, rows)
    field = field + beta * first_ref[...]
    field_ref[...] = field
    energy_ref[...] = jnp.zeros(energy_ref.shape, F32) + jnp.sum(scale_ref[...] * field * field)
    line = iota((8, 128), 0)
    scalar_ref[...] = jnp.where(line == 0, norm1, cross)


def lane_windows(band, rows):
    start = band * rows
    block, offset = start // 128, start % 128
    if offset + rows <= 128:
        return [(block, offset, offset + rows)]
    return [(block, offset, 128), (block + 1, 0, offset + rows - 128)]


def parity_row(wave, degrees):
    offset = iota((1, degrees), 1) - wave
    return jnp.where(offset >= 0, 1.0 - 2.0 * (offset & 1).astype(F32), 0.0)


def spectral_kernel(rows, with_base, owner_ref, order_ref, x_ref, basis_ref, spread_ref, *refs):
    if with_base:
        base_ref, across_ref, out_ref, send_ref, scalar_ref, stage_ref = refs
    else:
        out_ref, send_ref, across_ref, stage_ref = refs
    owned, half_rows, degrees = basis_ref.shape
    bands = half_rows // rows
    received = x_ref[...].astype(F32)
    lane = iota((1, 128), 1)
    if with_base:
        norm0, energy = unpack_scalars(received, 2)
        norm0 = (jnp.zeros((1, 1), F32) + norm0) * (1.0 / (2 * bands * 8))
        step_size = norm0 / (norm0 + energy)
        scalar_ref[...] = jnp.zeros((8, 128), F32) + step_size
    spread_rows = jnp.concatenate([spread_ref[...], spread_ref[...]], axis=0)
    stage_ref[...] = received
    senders = [stage_ref[pl.ds(place, 2 * bands * 8, stride=SUB), :] for place in range(SUB)]

    def along(place, group, side):
        columns = [jnp.zeros((8, 128), F32)] * (half_rows // 128)
        for band in range(bands):
            row = band if side == 0 else 2 * bands - 1 - band
            block = senders[place][8 * row : 8 * row + 8]
            shift = (rows * band - rows * group) % 128
            if shift:
                block = pltpu.roll(block, shift, 1)
            for index, low, high in lane_windows(band, rows):
                columns[index] = jnp.where((lane >= low) & (lane < high), block, columns[index])
        return jnp.concatenate(columns, axis=1)

    norm = jnp.zeros((16, degrees), F32)
    cross = jnp.zeros((16, degrees), F32)
    parities = []
    for slot in range(owned):
        parity = parity_row(order_ref[owner_ref[0] * owned + slot], degrees)
        parities.append(parity)
        pieces = [along(2 * (slot % 2) + r, slot // 2, side) for side in range(2) for r in range(2)]
        lhs = jnp.concatenate(pieces, axis=0).astype(BF)
        sums = mm(lhs, basis_ref[slot])
        if not with_base:
            across_ref[slot] = basis_ref[slot].T
        value = (sums[:16] * jnp.abs(parity) + parity * sums[16:]) * spread_rows
        if with_base:
            base = base_ref[slot]
            value = base - step_size * (base + value)
            cross = cross + value * base
        out_ref[slot] = value
        norm = norm + value * value
    if with_base:
        extra = pack_scalars([jnp.sum(norm), jnp.sum(cross)])
    else:
        extra = pack_scalars([jnp.sum(norm)])
    for slot in range(owned):
        parity = parities[slot]
        coeff = (out_ref[slot] * spread_rows * jnp.abs(parity)).astype(BF).astype(F32)
        even = jnp.where(parity > 0, coeff, 0.0)
        odd = jnp.where(parity < 0, coeff, 0.0)
        sums = mm(jnp.concatenate([even, odd], axis=0).astype(BF), across_ref[slot])
        sides = (sums[:16] + sums[16:], sums[:16] - sums[16:])
        group = slot // 2
        for side in range(2):
            for band in range(bands):
                row = band if side == 0 else 2 * bands - 1 - band
                for r in range(2):
                    lines = sides[side][8 * r : 8 * r + 8]
                    window = pl.ds(32 * row + 2 * (slot % 2) + r, 8, stride=SUB)
                    block = stage_ref[window, :] if group > 0 else jnp.zeros((8, 128), F32) + extra
                    shift = (rows * group - rows * band) % 128
                    start = rows * group
                    for index, low, high in lane_windows(band, rows):
                        source = lines[:, 128 * index : 128 * index + 128]
                        if shift:
                            source = pltpu.roll(source, shift, 1)
                        block = jnp.where((lane >= start) & (lane < start + high - low), source, block)
                        start += high - low
                    stage_ref[window, :] = block
    send_ref[...] = stage_ref[...].astype(BF)


def finish_kernel(energy_ref, norm0_ref, norms_ref, step_ref, rhs_ref, residual_ref, field1_ref, field2_ref,
                  control_ref, increment_ref):
    total = jnp.sum(energy_ref[...], axis=0, keepdims=True)[:, 0:1]
    first = norm0_ref[0:1, 0:1]
    norm1 = norms_ref[0:1, 0:1]
    cross = norms_ref[1:2, 0:1]
    step1 = step_ref[0:1, 0:1]
    beta = norm1 / first
    step2 = norm1 / (norm1 + 2.0 * beta * cross + beta * beta * first + total)
    mixed = step1 + step2 * beta
    for slot in range(rhs_ref.shape[0]):
        control_ref[slot] = mixed * rhs_ref[slot] + step2 * residual_ref[slot]
    increment_ref[...] = step1 * field1_ref[...] + step2 * field2_ref[...]


SMEM = pl.BlockSpec(memory_space=pltpu.SMEM)
VMEM = pl.BlockSpec(memory_space=pltpu.VMEM)
HBM = pl.BlockSpec(memory_space=pltpu.HBM)


def near(array):
    return pltpu.with_memory_space_constraint(array, pltpu.VMEM)


def far(array):
    return pltpu.with_memory_space_constraint(array, pltpu.HBM)


def shape(dims, dtype):
    return jax.ShapeDtypeStruct(dims, dtype)


def exchange(buffer):
    return lax.all_to_all(buffer, ("lat", "lev"), split_axis=0, concat_axis=0, tiled=True)


def local(innovation, obs_mask, obs_weight, order, basis, spread):
    lat = lax.axis_index("lat")
    lev = lax.axis_index("lev")
    devices = lax.axis_size("lat") * lax.axis_size("lev")
    owned, half_rows, degrees = basis.shape
    rows, points = innovation.shape[1:]
    chunk_rows = devices * SUB
    owner = (lat * lax.axis_size("lev") + lev).astype(jnp.int32).reshape(1)
    cols = order.reshape(devices, owned)
    table_rows = 2 * owned * devices
    stage = pltpu.VMEM((chunk_rows, 128), F32)
    rhs_part = pltpu.VMEM((256, points // 2), BF)
    plane = (rows, points)

    table, turn, basis, scale, send = pl.pallas_call(
        first_kernel,
        in_specs=[SMEM, VMEM, HBM, HBM, HBM, HBM],
        out_specs=[VMEM] * 5,
        out_shape=[
            pltpu.VMEM((table_rows, points // 4), BF),
            pltpu.VMEM((devices, 128), F32),
            pltpu.VMEM(basis.shape, BF),
            pltpu.VMEM(plane, F32),
            shape((chunk_rows, 128), BF),
        ],
        scratch_shapes=[pltpu.VMEM(plane, F32), pltpu.VMEM(plane, jnp.int32), pltpu.VMEM(plane, F32)]
        + [rhs_part, stage, pltpu.SemaphoreType.DMA((4,))],
        compiler_params=params(),
        name="first",
    )(owner, cols, *map(far, (innovation.reshape(plane), obs_mask.reshape(plane), obs_weight.reshape(plane), basis)))
    table, turn, basis, scale = map(near, (table, turn, basis, scale))

    def spectral(received, *more):
        with_base = len(more) > 0
        return pl.pallas_call(
            functools.partial(spectral_kernel, rows, with_base),
            in_specs=[SMEM, SMEM, VMEM, VMEM, VMEM] + [VMEM] * len(more),
            out_specs=[VMEM] * 3,
            out_shape=[shape((owned, 16, degrees), F32), shape((chunk_rows, 128), BF)]
            + [shape((8, 128), F32) if with_base else pltpu.VMEM((owned, degrees, half_rows), BF)],
            scratch_shapes=[stage],
            compiler_params=params(),
            name="spectral",
        )(owner, order, received, basis, spread, *more)

    rhs, send, across = spectral(exchange(send))
    across = near(across)
    field1, send, norm0 = pl.pallas_call(
        middle_kernel,
        in_specs=[SMEM, VMEM, VMEM, VMEM, VMEM],
        out_specs=[VMEM] * 3,
        out_shape=[shape(plane, F32), shape((chunk_rows, 128), BF), shape((8, 128), F32)],
        scratch_shapes=[rhs_part, stage],
        compiler_params=params(),
        name="middle",
    )(owner, exchange(send), table, turn, scale)
    residual, send, step1 = spectral(exchange(send), rhs, across)
    field2, energy, norms = pl.pallas_call(
        last_kernel,
        in_specs=[SMEM] + [VMEM] * 6,
        out_specs=[VMEM] * 3,
        out_shape=[shape(plane, F32), shape((devices, 128), F32), shape((8, 128), F32)],
        scratch_shapes=[stage],
        compiler_params=params(),
        name="last",
    )(owner, exchange(send), table, turn, scale, field1, norm0)
    control, increment = pl.pallas_call(
        finish_kernel,
        in_specs=[VMEM] * 8,
        out_specs=[VMEM] * 2,
        out_shape=[shape(rhs.shape, F32), shape(plane, F32)],
        compiler_params=params(),
        name="finish",
    )(exchange(energy), norm0, norms, step1, rhs, residual, field1, field2)
    return (control, increment.reshape(innovation.shape))


def solution(mesh):
    in_specs = (
        P("lev", "lat", None),
        P("lev", "lat", None),
        P("lev", "lat", None),
        P(),
        P(("lat", "lev"), None, None),
        P(),
    )
    out_specs = (P(("lat", "lev"), None, None), P("lev", "lat", None))
    return jax.shard_map(local, mesh=mesh, in_specs=in_specs, out_specs=out_specs, check_vma=False)
```
